256 devices in a mesh: seq: 64 (over z, x_hi, y), head: 4 (over x_lo, core).
Axes of the slice: x: 4 (x_hi: 2, x_lo: 2; x = x_hi * 2 + x_lo), y: 4, z: 8, core: 2. Of those that a mesh axis runs over, the one named last changes fastest.
Arguments:
- queries: bfloat16 [8192, 2560], P(('seq', 'head')), may hold values from -6 to 6
- keys: bfloat16 [8192, 2560], P(('seq', 'head')), may hold values from -6 to 6
- values: bfloat16 [8192, 2560], P(('seq', 'head')), may hold values from -6 to 6
- residual: bfloat16 [8192, 5120], P(('seq', 'head')), may hold values from -6 to 6
- cached_context: bfloat16 [8192, 2560], P('seq', 'head'), may hold values from -3 to 3
- out_weight_a: bfloat16 [2560, 5120], P('head'), may hold values from -0.125 to 0.125
- out_weight_b: bfloat16 [2560, 5120], P('head', 'seq'), may hold values from -0.125 to 0.125
- gate_a: float32 [5120], replicated, may hold values from 0.5 to 2
- gate_b: float32 [5120], replicated, may hold values from 0.5 to 2
Outputs:
- mixed: bfloat16 [8192, 5120], P(('seq', 'head'))
- attn_cache: bfloat16 [8192, 2560], P('seq', 'head')
The draws below stay inside these ranges and needn't reach their ends.
All inputs are finite; a program needn't handle non-finite values.
Results may differ from the reference program's by a relative error of at most 0.013.
Values may be sent and summed in bfloat16 or wider, within the bound.
A program may use at most 128 MiB of HBM per device.

```python
import math
import jax
import jax.numpy as jnp
from jax import lax

D = 5120
HEADS = 20
HD = 128
TOKENS = 8192


def draw_queries(key, part):
    key = jax.random.fold_in(key, 1)
    return (1.5 * jax.random.truncated_normal(key, -4.0, 4.0, (TOKENS, HEADS * HD), jnp.float32)).astype(jnp.bfloat16)


def draw_keys(key, part):
    key = jax.random.fold_in(key, 2)
    return (1.5 * jax.random.truncated_normal(key, -4.0, 4.0, (TOKENS, HEADS * HD), jnp.float32)).astype(jnp.bfloat16)


def shard_levels(stream_key, dims, cuts, least, high):
    level, own = 1.0, jax.random.fold_in(stream_key, 6)
    for axis_at, shards_of in cuts:
        steps = jnp.exp(jax.random.uniform(jax.random.fold_in(own, axis_at), (shards_of,), jnp.float32, least / len(cuts), high / len(cuts)))
        level = level * jnp.repeat(steps, dims[axis_at] // shards_of).reshape([-1 if axis == axis_at else 1 for axis in range(len(dims))])
    return level


def noise(key, dims, spread, limit, split=(), kind=jnp.bfloat16):
    values = jax.random.normal(key, dims, jnp.float32) * spread
    if len(split) > 0:
        values = shard_levels(key, dims, split, -0.22, 0.18) * values
    return jnp.clip(values, min=-limit, max=limit).astype(kind)


def setup_inputs(seed: int = 0) -> dict:
    seeds = jax.random.split(jax.random.key(seed), 10)
    queries = draw_queries(jax.random.fold_in(seeds[9], 71), 0)
    keys = draw_keys(jax.random.fold_in(seeds[9], 71), 0)
    values = noise(seeds[2], (TOKENS, HEADS * HD), 1.0, 6.0, ((0, 256),))
    residual = noise(seeds[3], (TOKENS, D), 1.0, 6.0, ((0, 256),))
    cached_context = noise(seeds[4], (TOKENS, HEADS * HD), 0.5, 3.0, ((0, 64), (1, 4)))
    out_weight_a = noise(seeds[5], (HEADS * HD, D), (HEADS * HD) ** -0.5, 0.125, ((0, 4),))
    out_weight_b = noise(seeds[6], (HEADS * HD, D), (HEADS * HD) ** -0.5, 0.125, ((0, 4), (1, 64)))
    gate_a = jnp.clip(jax.random.uniform(seeds[7], (D,), jnp.float32, 0.5, 2.0), 0.5, 2.0)
    gate_b = jnp.clip(jax.random.uniform(seeds[8], (D,), jnp.float32, 0.5, 2.0), 0.5, 2.0)
    return {"queries": queries, "keys": keys, "values": values, "residual": residual, "cached_context": cached_context, "out_weight_a": out_weight_a, "out_weight_b": out_weight_b, "gate_a": gate_a, "gate_b": gate_b}


def head_attention(query_head, key_head, value_head):
    block_rows = math.gcd(TOKENS, 1024)
    score_scale = 1.0 / math.sqrt(HD)

    def query_block(query_rows):
        scores = jnp.dot(query_rows, key_head.T, preferred_element_type=jnp.float32) * score_scale
        row_max = lax.optimization_barrier(jnp.max(scores, axis=1, keepdims=True))
        weights = jnp.exp(scores - row_max)
        row_sum = lax.optimization_barrier(jnp.sum(weights, axis=1, keepdims=True))
        context = jnp.dot(weights.astype(jnp.bfloat16), value_head, preferred_element_type=jnp.float32) / row_sum
        return context.astype(jnp.bfloat16)
    blocks = query_head.reshape(TOKENS // block_rows, block_rows, HD)
    return lax.map(query_block, blocks).reshape(TOKENS, HD)

def head_major(matrix):
    return matrix.reshape(TOKENS, HEADS, HD).transpose(1, 0, 2)

def per_head(triple):
    return head_attention(triple[0], triple[1], triple[2])

def reference(queries, keys, values, residual, cached_context, out_weight_a, out_weight_b, gate_a, gate_b):
    context = lax.map(per_head, (head_major(queries), head_major(keys), head_major(values)))
    attn_cache = context.transpose(1, 0, 2).reshape(TOKENS, HEADS * HD)
    branch_a = jnp.dot(attn_cache, out_weight_a, preferred_element_type=jnp.float32)
    branch_b = jnp.dot(cached_context, out_weight_b, preferred_element_type=jnp.float32)
    mixed = (residual.astype(jnp.float32) + gate_a * branch_a + gate_b * branch_b).astype(jnp.bfloat16)
    return (mixed, attn_cache)
```

```python
import math
import jax
import jax.numpy as jnp
from jax import lax
from jax.experimental import pallas as pl
from jax.experimental.pallas import tpu as pltpu
from jax.sharding import PartitionSpec as P

MESH = pl.DeviceIdType.MESH
BF = jnp.bfloat16
F32 = jnp.float32
HD = 128
EXP2_SCALE = math.log2(math.e) / math.sqrt(HD)


def place():
    s, h = lax.axis_index("seq"), lax.axis_index("head")
    return (s // 4) % 2 * 2 + h // 2, s % 4, s // 8, h % 2


def device(x, y, z, c):
    return (z * 8 + x // 2 * 4 + y, x % 2 * 2 + c)


def send(src, dst, ssem, rsem, to):
    return pltpu.make_async_remote_copy(
        src_ref=src, dst_ref=dst, send_sem=ssem, recv_sem=rsem, device_id=to, device_id_type=MESH
    )


def attention_kernel(
    q_in, k_in, v_in, cache_out,
    q_pack, kv_pack, kvm_pack, q_buf, kv, kvm, m_ref, l_ref, ot, o_buf, st_buf, o_rcv, m_rcv, st_rcv, stm_rcv, c_res, m_res, attn,
    xs_sem, xr_sem, ys_sem, yr_sem, zs_sem, zr_sem, os_sem, or_sem, bs_sem, br_sem,
):
    x, y, z, c = place()
    me = x * 2 + c
    up, down = device(x, y, (z + 1) % 8, c), device(x, y, (z + 7) % 8, c)
    x_peer = [None] + [(me + d) % 8 for d in range(1, 8)]
    x_dev = [None] + [device(p // 2, y, z, p % 2) for p in x_peer[1:]]

    barrier = pltpu.get_barrier_semaphore()
    peers = x_dev[1:] + [up, down]
    for d in range(1, 4):
        for cc in range(2):
            peers.append(device(x, (y + d) % 4, z, cc))
    for p in peers:
        pl.semaphore_signal(barrier, inc=1, device_id=p, device_id_type=MESH)

    for p in range(8):
        xx, cc = p // 2, p % 2
        heads = (5 * xx + 3 * cc, 5 * xx + 3 * cc + 1, 5 * xx + 2)
        for i, hh in enumerate(heads):
            cols = slice(hh * HD, (hh + 1) * HD)
            q_pack[p, i] = q_in[:, cols]
            if i < 2:
                kv_pack[p, i, 0] = k_in[:, cols]
                kv_pack[p, i, 1] = v_in[:, cols]
            elif cc == 0:
                kvm_pack[xx, 0] = k_in[:, cols]
                kvm_pack[xx, 1] = v_in[:, cols]
    q_buf[0, :, me] = q_pack[me]
    kv[0, :, me] = kv_pack[me]
    kvm[0, x] = kvm_pack[x]
    pl.semaphore_wait(barrier, len(peers))

    xq, xa, xb, xm = [], [], [], []
    for d in range(1, 8):
        xq.append(send(q_pack.at[x_peer[d]], q_buf.at[0, :, me], xs_sem.at[0, d], xr_sem.at[0, d], x_dev[d]))
        xq[-1].start()
    for i, l in ((0, xa), (1, xb)):
        for d in range(1, 8):
            l.append(send(kv_pack.at[x_peer[d], i], kv.at[0, i, me], xs_sem.at[1 + i, d], xr_sem.at[1 + i, d], x_dev[d]))
            l[-1].start()
    for d in range(1, 4):
        xx = (x + d) % 4
        xm.append(send(kvm_pack.at[xx], kvm.at[0, x], xs_sem.at[3, d], xr_sem.at[3, d], device(xx, y, z, c)))
        xm[-1].start()

    for cp in xq:
        cp.wait_recv()
    yq = []
    for d in range(1, 4):
        yq.append(send(q_buf.at[0], q_buf.at[d], ys_sem.at[d], yr_sem.at[d], device(x, (y + d) % 4, z, c)))
        yq[-1].start()

    def part_ref(part, slot):
        return kvm.at[slot] if part == 2 else kv.at[slot, part]

    def ring(part, step, way):
        src = 0 if step == 1 else 2 * (step - 1) - 1 + way
        dst = 7 if step == 4 else 2 * step - 1 + way
        return send(part_ref(part, src), part_ref(part, dst), zs_sem.at[part, step, way], zr_sem.at[part, step, way], (up, down)[way])

    rings = []
    def start_ring(part, step):
        ways = (0, 1) if step < 4 else ((0,) if part == 0 else (1,))
        for way in ways:
            cp = ring(part, step, way)
            cp.start()
            rings.append(cp)

    def wait_ring(part, step):
        ways = (0, 1) if step < 4 else ((0,) if part == 0 else (1,))
        for way in ways:
            ring(part, step, way).wait_recv()

    for part, l in ((0, xa), (1, xb), (2, xm)):
        for cp in l:
            cp.wait_recv()
        start_ring(part, 1)

    def attend(lo, n, first):
        for head in range(3):
            def tile(t, _):
                if head < 2:
                    kk = kv[lo:lo + n, head, :, 0].reshape(n * 256, HD)
                    vv = kv[lo:lo + n, head, :, 1].reshape(n * 256, HD)
                else:
                    kk = kvm[lo:lo + n, :, 0].reshape(n * 128, HD)
                    vv = kvm[lo:lo + n, :, 1].reshape(n * 128, HD)
                qq = q_buf[t, head].reshape(256, HD)
                s = lax.dot_general(kk, qq, (((1,), (1,)), ((), ())), preferred_element_type=F32)
                top = jnp.max(s, axis=0, keepdims=True)
                if not first:
                    old = m_ref[head, t]
                    top = jnp.maximum(top, old)
                    fade = jnp.exp2((old - top) * EXP2_SCALE)
                p = jnp.exp2(s * EXP2_SCALE - top * EXP2_SCALE)
                tot = jnp.sum(p, axis=0, keepdims=True)
                o = lax.dot_general(vv, p.astype(BF), (((0,), (0,)), ((), ())), preferred_element_type=F32)
                if first:
                    l_ref[head, t] = tot
                    ot[head, t] = o
                else:
                    l_ref[head, t] = l_ref[head, t] * fade + tot
                    ot[head, t] = ot[head, t] * fade + o
                m_ref[head, t] = top
                return 0
            lax.fori_loop(0, 4, tile, 0)

    for cp in yq:
        cp.wait_recv()
    attend(0, 1, True)
    for step in range(1, 5):
        for part in range(3):
            wait_ring(part, step)
            if step < 4:
                if step < 3 or True:
                    pass
                start_ring(part, step + 1)
        if step < 4:
            attend(2 * step - 1, 2, False)
    attend(7, 1, False)

    outs = []
    m_slot = c
    for t in (1, 2, 3, 0):
        for head in range(3):
            l = l_ref[head, t]
            o = (ot[head, t] / l).astype(BF)
            lse = m_ref[head, t] * EXP2_SCALE + jnp.log2(l)
            for half in range(2):
                cols = slice(half * HD, (half + 1) * HD)
                o_buf[t, half, head] = o[:, cols]
                st_buf[t, half, head:head + 1] = lse[:, cols]
        yy = (y + 4 - t) % 4
        same, other = device(x, yy, z, c), device(x, yy, z, 1 - c)
        if t > 0:
            outs.append(send(o_buf.at[t, :, 0:2], o_rcv.at[t], os_sem.at[t, 0], or_sem.at[t, 0], same))
            outs.append(send(st_buf.at[t], st_rcv.at[t], os_sem.at[t, 1], or_sem.at[t, 1], same))
            outs.append(send(o_buf.at[t, c, 2], m_rcv.at[t, 0], os_sem.at[t, 2], or_sem.at[t, 2], same))
        outs.append(send(o_buf.at[t, 1 - c, 2], m_rcv.at[t, 1], os_sem.at[t, 3], or_sem.at[t, 3], other))
        outs.append(send(st_buf.at[t, 1 - c], stm_rcv.at[t], os_sem.at[t, 4], or_sem.at[t, 4], other))
        for cp in outs[-(5 if t > 0 else 2):]:
            cp.start()
    for cp in outs:
        cp.wait_recv()

    def merge(parts):
        top = parts[0][1]
        for _, s in parts[1:]:
            top = jnp.maximum(top, s)
        acc, tot = 0.0, 0.0
        for o, s in parts:
            w = jnp.exp2(s - top)
            acc = acc + o.astype(F32) * w
            tot = tot + w
        return (acc / tot).T.astype(BF)

    for half in range(2):
        for head in range(2):
            parts = [(o_buf[0, half, head], st_buf[0, half, head:head + 1])]
            for d in range(1, 4):
                parts.append((o_rcv[d, half, head], st_rcv[d, half, head:head + 1]))
            c_res[half, head] = merge(parts)
    parts = [(o_buf[0, c, 2], st_buf[0, c, 2:3])]
    for d in range(4):
        if d > 0:
            parts.append((m_rcv[d, 0], st_rcv[d, c, 2:3]))
        parts.append((m_rcv[d, 1], stm_rcv[d, 2:3]))
    m_res[...] = merge(parts)

    def back(half):
        to_x, to_c = 2 * half + x // 2, x % 2
        own = (to_x == x) & (to_c == c)
        return own, device(to_x, y, z, to_c)

    ab = []
    for half in range(2):
        own, to = back(half)
        cp = send(c_res.at[half], attn.at[pl.ds(3 * c, 2)], bs_sem.at[half], br_sem.at[c], to)
        loc = pltpu.make_async_copy(c_res.at[half], attn.at[pl.ds(3 * c, 2)], br_sem.at[c])
        ab.append((own, cp))
        @pl.when(own)
        def _():
            loc.start()
        @pl.when(jnp.logical_not(own))
        def _():
            cp.start()
    to_x, to_c = 2 * c + x // 2, x % 2
    m_own = (to_x == x) & (to_c == c)
    mcp = send(m_res, attn.at[2], bs_sem.at[2], br_sem.at[2], device(to_x, y, z, to_c))
    mloc = pltpu.make_async_copy(m_res, attn.at[2], br_sem.at[2])
    @pl.when(m_own)
    def _():
        mloc.start()
    @pl.when(jnp.logical_not(m_own))
    def _():
        mcp.start()
    pltpu.make_async_copy(c_res.at[0], attn.at[0:2], br_sem.at[0]).wait()
    pltpu.make_async_copy(c_res.at[0], attn.at[3:5], br_sem.at[1]).wait()
    pltpu.make_async_copy(m_res, attn.at[2], br_sem.at[2]).wait()
    for i in range(5):
        cache_out[:, i * HD:(i + 1) * HD] = attn[i]

    for cp in xq + xa + xb + xm + yq + rings + outs:
        cp.wait_send()
    for own, cp in ab + [(m_own, mcp)]:
        @pl.when(jnp.logical_not(own))
        def _():
            cp.wait_send()


def attention(q, k, v):
    vm = pl.BlockSpec(memory_space=pltpu.VMEM)
    D = pltpu.SemaphoreType.DMA
    V = pltpu.VMEM
    return pl.pallas_call(
        attention_kernel,
        out_shape=jax.ShapeDtypeStruct((128, 640), BF),
        in_specs=[vm] * 3,
        out_specs=vm,
        scratch_shapes=[
            V((8, 3, 32, HD), BF), V((8, 2, 2, 32, HD), BF), V((4, 2, 32, HD), BF),
            V((4, 3, 8, 32, HD), BF),
            V((8, 2, 8, 2, 32, HD), BF), V((8, 4, 2, 32, HD), BF),
            V((3, 4, 1, 256), F32), V((3, 4, 1, 256), F32), V((3, 4, HD, 256), F32),
            V((4, 2, 3, HD, HD), BF), V((4, 2, 8, HD), F32),
            V((4, 2, 2, HD, HD), BF), V((4, 2, HD, HD), BF), V((4, 2, 8, HD), F32), V((4, 8, HD), F32),
            V((2, 2, HD, HD), BF), V((HD, HD), BF), V((5, HD, HD), BF),
            D((4, 8)), D((4, 8)), D((4,)), D((4,)), D((3, 5, 2)), D((3, 5, 2)), D((4, 5)), D((4, 5)), D((3,)), D((3,)),
        ],
        compiler_params=pltpu.CompilerParams(collective_id=1, has_side_effects=True, vmem_limit_bytes=48 * 2**20),
        name="attention",
    )(q, k, v)


def on_device(
    queries, keys, values, residual, cached_context, out_weight_a, out_weight_b, gate_a, gate_b
):
    attn_cache = attention(queries, keys, values)
    branch_b = jnp.dot(
        cached_context,
        lax.all_gather(out_weight_b, "seq", axis=1, tiled=True),
        preferred_element_type=F32,
    )
    first_rows = jnp.dot(attn_cache, out_weight_a, preferred_element_type=F32)
    summed = lax.psum_scatter(
        (gate_a * first_rows + gate_b * branch_b).astype(BF), "head", scatter_dimension=0, tiled=True
    ).astype(F32)
    mixed = (residual.astype(F32) + summed).astype(BF)
    return (mixed, attn_cache)


def solution(mesh):
    tokens = P(("seq", "head"), None)
    return jax.shard_map(
        on_device,
        mesh=mesh,
        in_specs=(tokens, tokens, tokens, tokens, P("seq", "head"), P("head", None), P("head", "seq"), P(), P()),
        out_specs=(tokens, P("seq", "head")),
        check_vma=False,
    )
```

```python
import math
import jax
import jax.numpy as jnp
from jax import lax
from jax.experimental import pallas as pl
from jax.experimental.pallas import tpu as pltpu
from jax.sharding import PartitionSpec as P

MESH = pl.DeviceIdType.MESH
BF = jnp.bfloat16
F32 = jnp.float32
HD = 128
EXP2_SCALE = math.log2(math.e) / math.sqrt(HD)


def place():
    s, h = lax.axis_index("seq"), lax.axis_index("head")
    return (s // 4) % 2 * 2 + h // 2, s % 4, s // 8, h % 2


def device(x, y, z, c):
    return (z * 8 + x // 2 * 4 + y, x % 2 * 2 + c)


def send(src, dst, ssem, rsem, to):
    return pltpu.make_async_remote_copy(
        src_ref=src, dst_ref=dst, send_sem=ssem, recv_sem=rsem, device_id=to, device_id_type=MESH
    )


def window_kernel(
    q_hbm, k_hbm, v_hbm, res_hbm, ctx_hbm, wa_hbm, wb_hbm, ga_hbm, gb_hbm, mixed_out, cache_out,
    q_in, k_in, v_in, res, wa, wb, ga, gb,
    q_pack, kv_pack, kvm_pack, q_buf, kv, kvm, m_ref, l_ref, ot, o_buf, st_buf, o_rcv, m_rcv, st_rcv, stm_rcv, c_res, m_res, attn,
    w_all, ctx, b_part, b_rcv1, b_snd2, b_keep, b_rcv2, b_snd3, b_rcv3, base,
    a_rows, p_snd1, p_keep1, p_rcv1, p_snd2, p_rcv2,
    in_sem, xs_sem, xr_sem, ys_sem, yr_sem, zs_sem, zr_sem, os_sem, or_sem, bs_sem, br_sem,
    ws_sem, wr_sem, cs_sem, cr_sem, ds_sem, dr_sem, ps_sem, pr_sem,
):
    x, y, z, c = place()
    me = x * 2 + c
    up, down = device(x, y, (z + 1) % 8, c), device(x, y, (z + 7) % 8, c)
    x_peer = [None] + [(me + d) % 8 for d in range(1, 8)]
    x_dev = [None] + [device(p // 2, y, z, p % 2) for p in x_peer[1:]]

    xl, xh = x % 2, x // 2
    core_dev, pair_dev = device(x, y, z, 1 - c), device(xh * 2 + 1 - xl, y, z, c)
    far_x = (1 - xh) * 2 + xl
    loads = []
    for i, (src, dst) in enumerate((
        (q_hbm, q_in), (k_hbm, k_in), (v_hbm, v_in), (wb_hbm, wb), (ctx_hbm, ctx.at[0, 0]),
        (gb_hbm, gb), (res_hbm, res), (ga_hbm, ga), (wa_hbm, wa),
    )):
        loads.append(pltpu.make_async_copy(src, dst, in_sem.at[i]))
        loads[-1].start()

    barrier = pltpu.get_barrier_semaphore()
    peers = x_dev[1:] + [up, down]
    for d in range(1, 4):
        for cc in range(2):
            peers.append(device(x, (y + d) % 4, z, cc))
        peers.append(device(far_x, (y + d) % 4, z, c))
    for p in peers:
        pl.semaphore_signal(barrier, inc=1, device_id=p, device_id_type=MESH)

    for cp in loads[0:4]:
        cp.wait()
    w_all[z] = wb[...].T
    for p in range(8):
        xx, cc = p // 2, p % 2
        heads = (5 * xx + 3 * cc, 5 * xx + 3 * cc + 1, 5 * xx + 2)
        for i, hh in enumerate(heads):
            cols = slice(hh * HD, (hh + 1) * HD)
            q_pack[p, i] = q_in[:, cols]
            if i < 2:
                kv_pack[p, i, 0] = k_in[:, cols]
                kv_pack[p, i, 1] = v_in[:, cols]
            elif cc == 0:
                kvm_pack[xx, 0] = k_in[:, cols]
                kvm_pack[xx, 1] = v_in[:, cols]
    q_buf[0, :, me] = q_pack[me]
    kv[0, :, me] = kv_pack[me]
    kvm[0, x] = kvm_pack[x]
    pl.semaphore_wait(barrier, len(peers))

    xq, xa, xb, xm = [], [], [], []
    for d in range(1, 8):
        xq.append(send(q_pack.at[x_peer[d]], q_buf.at[0, :, me], xs_sem.at[0, d], xr_sem.at[0, d], x_dev[d]))
        xq[-1].start()
    for i, l in ((0, xa), (1, xb)):
        for d in range(1, 8):
            l.append(send(kv_pack.at[x_peer[d], i], kv.at[0, i, me], xs_sem.at[1 + i, d], xr_sem.at[1 + i, d], x_dev[d]))
            l[-1].start()
    for d in range(1, 4):
        xx = (x + d) % 4
        xm.append(send(kvm_pack.at[xx], kvm.at[0, x], xs_sem.at[3, d], xr_sem.at[3, d], device(xx, y, z, c)))
        xm[-1].start()

    def w_ring(step, way):
        at = (z + 9 - step) % 8 if way == 0 else (z + 7 + step) % 8
        ref = w_all.at[at]
        if step == 4:
            ref = ref.at[0:48] if way == 0 else ref.at[48:80]
        return send(ref, ref, ws_sem.at[step, way], wr_sem.at[step, way], (up, down)[way])

    def w_start(step):
        for way in range(2):
            w_ring(step, way).start()

    def w_wait(step):
        for way in range(2):
            cp = w_ring(step, way)
            cp.wait_recv()
            cp.wait_send()

    w_start(1)

    for cp in xq:
        cp.wait_recv()
    yq = []
    for d in range(1, 4):
        yq.append(send(q_buf.at[0], q_buf.at[d], ys_sem.at[d], yr_sem.at[d], device(x, (y + d) % 4, z, c)))
        yq[-1].start()

    loads[4].wait()
    ctx_x = send(ctx.at[0, 0], ctx.at[0, 1], cs_sem.at[0], cr_sem.at[0], device(far_x, y, z, c))
    ctx_x.start()
    w_wait(1)
    w_start(2)

    def part_ref(part, slot):
        return kvm.at[slot] if part == 2 else kv.at[slot, part]

    def ring(part, step, way):
        src = 0 if step == 1 else 2 * (step - 1) - 1 + way
        dst = 7 if step == 4 else 2 * step - 1 + way
        return send(part_ref(part, src), part_ref(part, dst), zs_sem.at[part, step, way], zr_sem.at[part, step, way], (up, down)[way])

    rings = []
    def start_ring(part, step):
        ways = (0, 1) if step < 4 else ((0,) if part == 0 else (1,))
        for way in ways:
            cp = ring(part, step, way)
            cp.start()
            rings.append(cp)

    def wait_ring(part, step):
        ways = (0, 1) if step < 4 else ((0,) if part == 0 else (1,))
        for way in ways:
            ring(part, step, way).wait_recv()

    for part, l in ((0, xa), (1, xb), (2, xm)):
        for cp in l:
            cp.wait_recv()
        start_ring(part, 1)

    def attend(lo, n, first):
        for head in range(3):
            def tile(t, _):
                if head < 2:
                    kk = kv[lo:lo + n, head, :, 0].reshape(n * 256, HD)
                    vv = kv[lo:lo + n, head, :, 1].reshape(n * 256, HD)
                else:
                    kk = kvm[lo:lo + n, :, 0].reshape(n * 128, HD)
                    vv = kvm[lo:lo + n, :, 1].reshape(n * 128, HD)
                qq = q_buf[t, head].reshape(256, HD)
                s = lax.dot_general(kk, qq, (((1,), (1,)), ((), ())), preferred_element_type=F32)
                top = jnp.max(s, axis=0, keepdims=True)
                if not first:
                    old = m_ref[head, t]
                    top = jnp.maximum(top, old)
                    fade = jnp.exp2((old - top) * EXP2_SCALE)
                p = jnp.exp2(s * EXP2_SCALE - top * EXP2_SCALE)
                tot = jnp.sum(p, axis=0, keepdims=True)
                o = lax.dot_general(vv, p.astype(BF), (((0,), (0,)), ((), ())), preferred_element_type=F32)
                if first:
                    l_ref[head, t] = tot
                    ot[head, t] = o
                else:
                    l_ref[head, t] = l_ref[head, t] * fade + tot
                    ot[head, t] = ot[head, t] * fade + o
                m_ref[head, t] = top
                return 0
            lax.fori_loop(0, 4, tile, 0)

    w_wait(2)
    w_start(3)
    for cp in yq:
        cp.wait_recv()
    ctx_x.wait_recv()
    ctx_y = []
    for d in range(1, 4):
        ctx_y.append(send(ctx.at[0], ctx.at[d], cs_sem.at[d], cr_sem.at[d], device(x, (y + d) % 4, z, c)))
        ctx_y[-1].start()
    w_wait(3)
    w_start(4)
    attend(0, 1, True)
    for step in range(1, 5):
        for part in range(3):
            wait_ring(part, step)
            if step < 4:
                start_ring(part, step + 1)
        if step < 4:
            attend(2 * step - 1, 2, False)
        if step == 3:
            w_wait(4)
            for cp in ctx_y:
                cp.wait_recv()

            def b_tile(d, _):
                part = lax.dot_general(
                    ctx[d].reshape(256, 640), w_all[...].reshape(640, 640),
                    (((1,), (1,)), ((), ())), preferred_element_type=F32,
                )
                b_part[d] = part.astype(BF).reshape(2, 2, 2, 32, 640)
                return 0
            lax.fori_loop(0, 4, b_tile, 0)
            b_core = send(b_part.at[:, :, :, 1 - c], b_rcv1, ds_sem.at[0], dr_sem.at[0], core_dev)
            b_core.start()
    attend(7, 1, False)

    outs = []
    m_slot = c
    for t in (1, 2, 3, 0):
        for head in range(3):
            l = l_ref[head, t]
            o = (ot[head, t] / l).astype(BF)
            lse = m_ref[head, t] * EXP2_SCALE + jnp.log2(l)
            for half in range(2):
                cols = slice(half * HD, (half + 1) * HD)
                o_buf[t, half, head] = o[:, cols]
                st_buf[t, half, head:head + 1] = lse[:, cols]
        yy = (y + 4 - t) % 4
        same, other = device(x, yy, z, c), device(x, yy, z, 1 - c)
        if t > 0:
            outs.append(send(o_buf.at[t, :, 0:2], o_rcv.at[t], os_sem.at[t, 0], or_sem.at[t, 0], same))
            outs.append(send(st_buf.at[t], st_rcv.at[t], os_sem.at[t, 1], or_sem.at[t, 1], same))
            outs.append(send(o_buf.at[t, c, 2], m_rcv.at[t, 0], os_sem.at[t, 2], or_sem.at[t, 2], same))
        outs.append(send(o_buf.at[t, 1 - c, 2], m_rcv.at[t, 1], os_sem.at[t, 3], or_sem.at[t, 3], other))
        outs.append(send(st_buf.at[t, 1 - c], stm_rcv.at[t], os_sem.at[t, 4], or_sem.at[t, 4], other))
        for cp in outs[-(5 if t > 0 else 2):]:
            cp.start()
    b_core.wait_recv()

    def b_sum1(d, _):
        for e in range(2):
            b_snd2[d, e] = (b_part[d, e, 1 - xl, c].astype(F32) + b_rcv1[d, e, 1 - xl].astype(F32)).astype(BF)
            b_keep[d, e] = b_part[d, e, xl, c].astype(F32) + b_rcv1[d, e, xl].astype(F32)
        return 0
    lax.fori_loop(0, 4, b_sum1, 0)
    b_pair = send(b_snd2, b_rcv2, ds_sem.at[1], dr_sem.at[1], pair_dev)
    b_pair.start()

    for cp in outs:
        cp.wait_recv()

    def merge(parts):
        top = parts[0][1]
        for _, s in parts[1:]:
            top = jnp.maximum(top, s)
        acc, tot = 0.0, 0.0
        for o, s in parts:
            w = jnp.exp2(s - top)
            acc = acc + o.astype(F32) * w
            tot = tot + w
        return (acc / tot).T.astype(BF)

    for half in range(2):
        for head in range(2):
            parts = [(o_buf[0, half, head], st_buf[0, half, head:head + 1])]
            for d in range(1, 4):
                parts.append((o_rcv[d, half, head], st_rcv[d, half, head:head + 1]))
            c_res[half, head] = merge(parts)
    parts = [(o_buf[0, c, 2], st_buf[0, c, 2:3])]
    for d in range(4):
        if d > 0:
            parts.append((m_rcv[d, 0], st_rcv[d, c, 2:3]))
        parts.append((m_rcv[d, 1], stm_rcv[d, 2:3]))
    m_res[...] = merge(parts)

    def back(half):
        to_x, to_c = 2 * half + x // 2, x % 2
        own = (to_x == x) & (to_c == c)
        return own, device(to_x, y, z, to_c)

    ab = []
    for half in range(2):
        own, to = back(half)
        cp = send(c_res.at[half], attn.at[pl.ds(3 * c, 2)], bs_sem.at[half], br_sem.at[c], to)
        loc = pltpu.make_async_copy(c_res.at[half], attn.at[pl.ds(3 * c, 2)], br_sem.at[c])
        ab.append((own, cp))
        @pl.when(own)
        def _():
            loc.start()
        @pl.when(jnp.logical_not(own))
        def _():
            cp.start()
    to_x, to_c = 2 * c + x // 2, x % 2
    m_own = (to_x == x) & (to_c == c)
    mcp = send(m_res, attn.at[2], bs_sem.at[2], br_sem.at[2], device(to_x, y, z, to_c))
    mloc = pltpu.make_async_copy(m_res, attn.at[2], br_sem.at[2])
    @pl.when(m_own)
    def _():
        mloc.start()
    @pl.when(jnp.logical_not(m_own))
    def _():
        mcp.start()
    b_pair.wait_recv()

    def b_sum2(d, _):
        for e in range(2):
            b_snd3[d, e] = (b_keep[d, e] + b_rcv2[d, e].astype(F32)).astype(BF)
        return 0
    lax.fori_loop(0, 4, b_sum2, 0)
    q_me = xh * 4 + y
    b_out = []
    for d in range(4):
        for e in range(2):
            if d + e > 0:
                to = device(far_x if e else x, (y + 4 - d) % 4, z, c)
                b_out.append(send(b_snd3.at[d, e], b_rcv3.at[q_me], ds_sem.at[2 + 2 * d + e], dr_sem.at[2 + 2 * d + e], to))
                b_out[-1].start()
    b_rcv3[q_me] = b_snd3[0, 0]
    pltpu.make_async_copy(c_res.at[0], attn.at[0:2], br_sem.at[0]).wait()
    pltpu.make_async_copy(c_res.at[0], attn.at[3:5], br_sem.at[1]).wait()
    pltpu.make_async_copy(m_res, attn.at[2], br_sem.at[2]).wait()
    for i in range(5):
        cache_out[:, i * HD:(i + 1) * HD] = attn[i]

    for i, (pl_x, pl_c) in enumerate(((1 - xl, 1 - c), (xl, 1 - c), (1 - xl, c), (xl, c))):
        for head in range(5):
            a_rows[i * 32:(i + 1) * 32, head * HD:(head + 1) * HD] = attn[head, pl.ds((pl_x * 2 + pl_c) * 32, 32)]
    loads[8].wait()
    stage1, stage2 = [], []
    for j in range(5):
        cols = slice(j * 1024, (j + 1) * 1024)
        part = jnp.dot(a_rows[...], wa[:, cols], preferred_element_type=F32)
        p_snd1[j] = part[0:64].astype(BF)
        stage1.append(send(p_snd1.at[j], p_rcv1.at[j], ps_sem.at[0, j], pr_sem.at[0, j], core_dev))
        stage1[-1].start()
        p_keep1[j] = part[64:128]
    for j in range(5):
        stage1[j].wait_recv()
        p_snd2[j] = (p_keep1[j, 0:32] + p_rcv1[j, 0:32].astype(F32)).astype(BF)
        stage2.append(send(p_snd2.at[j], p_rcv2.at[j], ps_sem.at[1, j], pr_sem.at[1, j], pair_dev))
        stage2[-1].start()

    for cp in b_out:
        cp.wait_recv()
    for cp in loads[5:8]:
        cp.wait()
    for zz in range(8):
        cols = slice(zz * 640, (zz + 1) * 640)
        piece = jnp.concatenate([b_rcv3[qq, :, zz * 80:(zz + 1) * 80].astype(F32) for qq in range(8)], axis=1)
        base[:, cols] = res[:, cols].astype(F32) + gb[:, cols] * piece
    for j in range(5):
        cols = slice(j * 1024, (j + 1) * 1024)
        stage2[j].wait_recv()
        total = p_keep1[j, 32:64] + p_rcv1[j, 32:64].astype(F32) + p_rcv2[j].astype(F32)
        mixed_out[:, cols] = (base[:, cols] + ga[:, cols] * total).astype(BF)

    for cp in xq + xa + xb + xm + yq + rings + outs + [ctx_x, b_core, b_pair] + ctx_y + b_out + stage1 + stage2:
        cp.wait_send()
    for own, cp in ab + [(m_own, mcp)]:
        @pl.when(jnp.logical_not(own))
        def _():
            cp.wait_send()


def window(q, k, v, res, ctx, wa, wb, ga, gb):
    any_space = pl.BlockSpec(memory_space=pl.ANY)
    vm = pl.BlockSpec(memory_space=pltpu.VMEM)
    D = pltpu.SemaphoreType.DMA
    V = pltpu.VMEM
    return pl.pallas_call(
        window_kernel,
        out_shape=(jax.ShapeDtypeStruct((32, 5120), BF), jax.ShapeDtypeStruct((128, 640), BF)),
        in_specs=[any_space] * 9,
        out_specs=(vm, vm),
        scratch_shapes=[
            V((32, 2560), BF), V((32, 2560), BF), V((32, 2560), BF), V((32, 5120), BF),
            V((640, 5120), BF), V((640, 80), BF), V((1, 5120), F32), V((1, 5120), F32),
            V((8, 3, 32, HD), BF), V((8, 2, 2, 32, HD), BF), V((4, 2, 32, HD), BF),
            V((4, 3, 8, 32, HD), BF),
            V((8, 2, 8, 2, 32, HD), BF), V((8, 4, 2, 32, HD), BF),
            V((3, 4, 1, 256), F32), V((3, 4, 1, 256), F32), V((3, 4, HD, 256), F32),
            V((4, 2, 3, HD, HD), BF), V((4, 2, 8, HD), F32),
            V((4, 2, 2, HD, HD), BF), V((4, 2, HD, HD), BF), V((4, 2, 8, HD), F32), V((4, 8, HD), F32),
            V((2, 2, HD, HD), BF), V((HD, HD), BF), V((5, HD, HD), BF),
            V((8, 80, 640), BF), V((4, 2, HD, 640), BF), V((4, 2, 2, 2, 32, 640), BF), V((4, 2, 2, 32, 640), BF),
            V((4, 2, 32, 640), BF), V((4, 2, 32, 640), F32), V((4, 2, 32, 640), BF), V((4, 2, 32, 640), BF),
            V((8, 32, 640), BF), V((32, 5120), F32),
            V((HD, 640), BF), V((5, 64, 1024), BF), V((5, 64, 1024), F32), V((5, 64, 1024), BF),
            V((5, 32, 1024), BF), V((5, 32, 1024), BF),
            D((9,)), D((4, 8)), D((4, 8)), D((4,)), D((4,)), D((3, 5, 2)), D((3, 5, 2)), D((4, 5)), D((4, 5)),
            D((3,)), D((3,)), D((5, 2)), D((5, 2)), D((4,)), D((4,)), D((10,)), D((10,)), D((2, 5)), D((2, 5)),
        ],
        compiler_params=pltpu.CompilerParams(collective_id=1, has_side_effects=True, vmem_limit_bytes=56 * 2**20),
        name="window",
    )(q, k, v, res, ctx, wa, wb, ga.reshape(1, 5120), gb.reshape(1, 5120))


def solution(mesh):
    tokens = P(("seq", "head"), None)
    return jax.shard_map(
        window,
        mesh=mesh,
        in_specs=(tokens, tokens, tokens, tokens, P("seq", "head"), P("head", None), P("head", "seq"), P(), P()),
        out_specs=(tokens, P("seq", "head")),
        check_vma=False,
    )
```

```python
import math

import jax
import jax.numpy as jnp
from jax import lax
from jax.experimental import pallas as pl
from jax.experimental.pallas import tpu as pltpu
from jax.sharding import PartitionSpec as P

MESH = pl.DeviceIdType.MESH
BF = jnp.bfloat16
F32 = jnp.float32
HD = 128
EXP2_SCALE = math.log2(math.e) / math.sqrt(HD)


def place():
    s, h = lax.axis_index("seq"), lax.axis_index("head")
    return (s // 4) % 2 * 2 + h // 2, s % 4, s // 8, h % 2


def device(x, y, z, c):
    return (z * 8 + x // 2 * 4 + y, x % 2 * 2 + c)


def send(src, dst, ssem, rsem, to):
    return pltpu.make_async_remote_copy(
        src_ref=src, dst_ref=dst, send_sem=ssem, recv_sem=rsem, device_id=to, device_id_type=MESH
    )


def window_kernel(
    q_hbm, k_hbm, v_hbm, res_hbm, ctx_hbm, wa_hbm, wb_hbm, ga_hbm, gb_hbm, mixed_out, cache_out,
    q_in, k_in, v_in, res, wa, ga, gb,
    q_pack, kv_pack, kvm_pack, q_buf, kv, kvm, m_ref, l_ref, ot, o_buf, st_buf, o_rcv, m_rcv, st_rcv, stm_rcv, c_res, m_res, attn,
    w_all, ctx, b_part, b_rcv1, b_snd2, b_keep, b_rcv2, b_snd3, b_rcvx, b_rcv3, base,
    a_rows, p_pre, p_snd1, p_keep1, p_rcv1, p_snd2, p_rcv2,
    in_sem, xs_sem, xr_sem, ys_sem, yr_sem, zs_sem, zr_sem, os_sem, or_sem, bs_sem, br_sem,
    ws_sem, wr_sem, cs_sem, cr_sem, ds_sem, dr_sem, ps_sem, pr_sem,
):
    x, y, z, c = place()
    me = x * 2 + c
    xl, xh = x % 2, x // 2
    up, down = device(x, y, (z + 1) % 8, c), device(x, y, (z + 7) % 8, c)
    core_dev, pair_dev = device(x, y, z, 1 - c), device(xh * 2 + 1 - xl, y, z, c)
    far_x = (1 - xh) * 2 + xl
    x_peer = [None] + [(me + d) % 8 for d in range(1, 8)]
    x_dev = [None] + [device(p // 2, y, z, p % 2) for p in x_peer[1:]]
    sent = []

    def go(cp):
        cp.start()
        sent.append(cp)
        return cp

    loads = []
    for i, (src, dst) in enumerate((
        (k_hbm, k_in), (v_hbm, v_in), (q_hbm, q_in), (wb_hbm, w_all.at[z]), (ctx_hbm, ctx.at[0, 0]),
        (gb_hbm, gb), (res_hbm, res), (ga_hbm, ga), (wa_hbm, wa),
    )):
        loads.append(pltpu.make_async_copy(src, dst, in_sem.at[i]))
        if i < 8:
            loads[-1].start()

    barrier = pltpu.get_barrier_semaphore()
    peers = x_dev[1:] + [up, down]
    for d in range(1, 4):
        for cc in range(2):
            peers.append(device(x, (y + d) % 4, z, cc))
    for p in peers:
        pl.semaphore_signal(barrier, inc=1, device_id=p, device_id_type=MESH)

    for cp in loads[0:3]:
        cp.wait()
    for p in range(8):
        xx, cc = p // 2, p % 2
        heads = (5 * xx + 3 * cc, 5 * xx + 3 * cc + 1, 5 * xx + 2)
        for i, hh in enumerate(heads):
            cols = slice(hh * HD, (hh + 1) * HD)
            q_pack[p, i] = q_in[:, cols]
            if i < 2:
                kv_pack[p, i, 0] = k_in[:, cols]
                kv_pack[p, i, 1] = v_in[:, cols]
            elif cc == 0:
                kvm_pack[xx, 0] = k_in[:, cols]
                kvm_pack[xx, 1] = v_in[:, cols]
    q_buf[0, :, me] = q_pack[me]
    kv[0, :, me] = kv_pack[me]
    kvm[0, x] = kvm_pack[x]
    pl.semaphore_wait(barrier, len(peers))


    x_kv = [[], [], []]
    for i in range(2):
        for d in range(1, 8):
            x_kv[i].append(go(send(
                kv_pack.at[x_peer[d], i], kv.at[0, i, me], xs_sem.at[1 + i, d], xr_sem.at[1 + i, d], x_dev[d])))
    for d in range(1, 4):
        xx = (x + d) % 4
        x_kv[2].append(go(send(
            kvm_pack.at[xx], kvm.at[0, x], xs_sem.at[3, d], xr_sem.at[3, d], device(xx, y, z, c))))
    loads[8].start()
    x_q = []
    for d in range(1, 8):
        x_q.append(go(send(q_pack.at[x_peer[d]], q_buf.at[0, :, me], xs_sem.at[0, d], xr_sem.at[0, d], x_dev[d])))

    def w_ring(step, way):
        at = (z + 9 - step) % 8 if way == 0 else (z + 7 + step) % 8
        ref = w_all.at[at]
        if step == 4:
            ref = ref.at[0:48] if way == 0 else ref.at[48:80]
        return send(ref, ref, ws_sem.at[step, way], wr_sem.at[step, way], (up, down)[way])

    rings = {}

    def w_start(step):
        for way in range(2):
            rings[step, way] = go(w_ring(step, way))

    def w_wait(step):
        for way in range(2):
            rings[step, way].wait_recv()

    loads[3].wait()
    w_start(1)

    ctx_y = []
    loads[4].wait()
    for d in range(1, 4):
        ctx_y.append(go(send(ctx.at[0, 0], ctx.at[d, 0], cs_sem.at[d], cr_sem.at[d], device(x, (y + d) % 4, z, c))))
    w_wait(1)
    w_start(2)

    def part_ref(part, slot):
        return kvm.at[slot] if part == 2 else kv.at[slot, part]

    def ring(part, step, way):
        src = 0 if step == 1 else 2 * (step - 1) - 1 + way
        dst = 7 if step == 4 else 2 * step - 1 + way
        return send(
            part_ref(part, src), part_ref(part, dst), zs_sem.at[part, step, way], zr_sem.at[part, step, way], (up, down)[way])

    def ways_of(part, step):
        return (0, 1) if step < 4 else ((0,) if part == 0 else (1,))

    def ring_start(part, step):
        for way in ways_of(part, step):
            rings[part, step, way] = go(ring(part, step, way))

    def ring_next(part, step):
        for way in ways_of(part, step):
            rings[part, step, way].wait_recv()
        if step < 4:
            ring_start(part, step + 1)

    for part in range(3):
        for cp in x_kv[part]:
            cp.wait_recv()
        ring_start(part, 1)

    for cp in x_q:
        cp.wait_recv()
    y_q = []
    for d in range(1, 4):
        y_q.append(go(send(q_buf.at[0], q_buf.at[d], ys_sem.at[d], yr_sem.at[d], device(x, (y + d) % 4, z, c))))
    ctx_x = []
    for d in range(4):
        if d > 0:
            ctx_y[d - 1].wait_recv()
        ctx_x.append(go(send(ctx.at[d, 0], ctx.at[d, 1], cs_sem.at[4 + d], cr_sem.at[4 + d], device(far_x, y, z, c))))
    w_wait(2)
    w_start(3)

    def attend(head, lo, n, first=False, last=False):
        if head < 2:
            kk = kv[lo:lo + n, head, :, 0].reshape(n * 256, HD)
            vv = kv[lo:lo + n, head, :, 1].reshape(n * 256, HD)
        else:
            kk = kvm[lo:lo + n, :, 0].reshape(n * 128, HD)
            vv = kvm[lo:lo + n, :, 1].reshape(n * 128, HD)

        def scores(t):
            return lax.dot_general(
                kk, q_buf[t, head].reshape(256, HD), (((1,), (1,)), ((), ())), preferred_element_type=F32)

        def rest(t, s):
            top = jnp.max(s, axis=0, keepdims=True)
            if not first:
                old = m_ref[head, t]
                top = jnp.maximum(top, old)
                fade = jnp.exp2((old - top) * EXP2_SCALE)
            p = jnp.exp2(s * EXP2_SCALE - top * EXP2_SCALE)
            tot = jnp.sum(p, axis=0, keepdims=True)
            o = lax.dot_general(vv, p.astype(BF), (((0,), (0,)), ((), ())), preferred_element_type=F32)
            if not first:
                tot = l_ref[head, t] * fade + tot
                o = ot[head, t] * fade + o
            if last:
                o = (o * (1.0 / tot)).astype(BF)
                lse = top * EXP2_SCALE + jnp.log2(tot)
                for half in range(2):
                    cols = slice(half * HD, (half + 1) * HD)
                    o_buf[t, head, half] = o[:, cols]
                    st_buf[t, head, half, 0:1] = lse[:, cols]
            else:
                l_ref[head, t] = tot
                ot[head, t] = o
                m_ref[head, t] = top

        order = (1, 2, 3, 0)
        following = scores(order[0])
        for i, t in enumerate(order):
            current = following
            if i < 3:
                following = scores(order[i + 1])
            rest(t, current)

    for part in range(3):
        ring_next(part, 1)
    w_wait(3)
    w_start(4)
    for cp in y_q:
        cp.wait_recv()

    for part in range(3):
        attend(part, 0, 1, first=True)
    for part in range(3):
        ring_next(part, 2)
        attend(part, 1, 2)

    w_wait(4)
    for cp in ctx_x:
        cp.wait_recv()

    def b_tile(d, _):
        part = lax.dot_general(
            ctx[d].reshape(256, 640), w_all[...].reshape(640, 640),
            (((1,), (1,)), ((), ())), preferred_element_type=F32,
        )
        b_part[d] = part.astype(BF).reshape(2, 2, 2, 32, 640)
        return 0
    lax.fori_loop(0, 4, b_tile, 0)
    b_core = go(send(b_part.at[:, :, :, 1 - c], b_rcv1, ds_sem.at[0], dr_sem.at[0], core_dev))
    attend(0, 3, 2)
    ring_next(0, 3)
    attend(1, 3, 2)
    ring_next(1, 3)
    attend(2, 3, 2)
    ring_next(2, 3)
    b_core.wait_recv()

    def b_sum1(d, _):
        for e in range(2):
            b_snd2[e, d] = (b_part[d, e, 1 - xl, c].astype(F32) + b_rcv1[d, e, 1 - xl].astype(F32)).astype(BF)
            b_keep[e, d] = b_part[d, e, xl, c].astype(F32) + b_rcv1[d, e, xl].astype(F32)
        return 0
    lax.fori_loop(0, 4, b_sum1, 0)
    b_pair = go(send(b_snd2, b_rcv2, ds_sem.at[1], dr_sem.at[1], pair_dev))
    for part in range(3):
        attend(part, 5, 2)

    outs = [[], [], []]
    for head in range(3):
        ring_next(head, 4)
        attend(head, 7, 1, last=True)
        for t in (1, 2, 3, 0):
            yy = (y + 4 - t) % 4
            same, other = device(x, yy, z, c), device(x, yy, z, 1 - c)

            def out(src, dst, i, to):
                outs[head].append(go(send(src, dst, os_sem.at[t, i], or_sem.at[t, i], to)))

            if head < 2 and t > 0:
                out(o_buf.at[t, head], o_rcv.at[t, head], 2 * head, same)
                out(st_buf.at[t, head], st_rcv.at[t, head], 2 * head + 1, same)
            elif head == 2:
                if t > 0:
                    out(o_buf.at[t, 2, c], m_rcv.at[t, 0], 4, same)
                    out(st_buf.at[t, 2, c], stm_rcv.at[t, 0], 5, same)
                out(o_buf.at[t, 2, 1 - c], m_rcv.at[t, 1], 6, other)
                out(st_buf.at[t, 2, 1 - c], stm_rcv.at[t, 1], 7, other)

    b_pair.wait_recv()

    def b_sum2(d, _):
        for e in range(2):
            b_snd3[e, d] = (b_keep[e, d] + b_rcv2[e, d].astype(F32)).astype(BF)
        return 0
    lax.fori_loop(0, 4, b_sum2, 0)
    b_x = go(send(b_snd3.at[1], b_rcvx, ds_sem.at[2], dr_sem.at[2], device(far_x, y, z, c)))

    def merge(parts):
        top = parts[0][1]
        for _, s in parts[1:]:
            top = jnp.maximum(top, s)
        acc, tot = 0.0, 0.0
        for o, s in parts:
            w = jnp.exp2(s - top)
            acc = acc + o.astype(F32) * w
            tot = tot + w
        return (acc * (1.0 / tot)).T.astype(BF)

    back = []

    def give(src, head, sem, to_x, rsem):
        own = (to_x == x) & (x % 2 == c)
        cp = send(src, attn.at[head], bs_sem.at[sem], br_sem.at[rsem], device(to_x, y, z, x % 2))
        loc = pltpu.make_async_copy(src, attn.at[head], br_sem.at[rsem])

        @pl.when(own)
        def _():
            loc.start()

        @pl.when(jnp.logical_not(own))
        def _():
            cp.start()
        back.append((own, cp))

    for head in range(2):
        for cp in outs[head]:
            cp.wait_recv()
        for half in range(2):
            parts = [(o_buf[0, head, half], st_buf[0, head, half, 0:1])]
            for d in range(1, 4):
                parts.append((o_rcv[d, head, half], st_rcv[d, head, half, 0:1]))
            c_res[head, half] = merge(parts)
            give(c_res.at[head, half], 3 * c + head, 2 * head + half, 2 * half + x // 2, 3 * c + head)
    for cp in outs[2]:
        cp.wait_recv()
    parts = [(o_buf[0, 2, c], st_buf[0, 2, c, 0:1])]
    for d in range(4):
        if d > 0:
            parts.append((m_rcv[d, 0], stm_rcv[d, 0, 0:1]))
        parts.append((m_rcv[d, 1], stm_rcv[d, 1, 0:1]))
    m_res[...] = merge(parts)
    give(m_res, 2, 4, 2 * c + x // 2, 2)

    b_x.wait_recv()
    q_me, q_far = xh * 4 + y, (1 - xh) * 4 + y
    b_out = []
    for d in range(1, 4):
        to = device(x, (y + 4 - d) % 4, z, c)
        b_out.append(go(send(b_snd3.at[0, d], b_rcv3.at[q_me], ds_sem.at[2 + d], dr_sem.at[2 + d], to)))
        b_out.append(go(send(b_rcvx.at[d], b_rcv3.at[q_far], ds_sem.at[5 + d], dr_sem.at[5 + d], to)))
    b_rcv3[q_me] = b_snd3[0, 0]
    b_rcv3[q_far] = b_rcvx[0]

    def take(head):
        pltpu.make_async_copy(m_res, attn.at[head], br_sem.at[head]).wait()
        cache_out[:, head * HD:(head + 1) * HD] = attn[head]
        for i, (row_x, row_c) in enumerate(((1 - xl, 1 - c), (xl, 1 - c), (1 - xl, c), (xl, c))):
            a_rows[i * 32:(i + 1) * 32, head * HD:(head + 1) * HD] = attn[head, pl.ds((row_x * 2 + row_c) * 32, 32)]

    for head in (0, 1, 3, 4):
        take(head)
    loads[8].wait()
    for j in range(5):
        cols = slice(j * 1024, (j + 1) * 1024)
        p_pre[:, cols] = (
            jnp.dot(a_rows[:, 0:256], wa[0:256, cols], preferred_element_type=F32)
            + jnp.dot(a_rows[:, 384:640], wa[384:640, cols], preferred_element_type=F32)
        )
    take(2)
    stage1, stage2 = [], []
    for j in range(5):
        cols = slice(j * 1024, (j + 1) * 1024)
        part = jnp.dot(a_rows[:, 256:384], wa[256:384, cols], preferred_element_type=F32) + p_pre[:, cols]
        p_snd1[j] = part[0:64].astype(BF)
        stage1.append(go(send(p_snd1.at[j], p_rcv1.at[j], ps_sem.at[0, j], pr_sem.at[0, j], core_dev)))
        p_keep1[j] = part[64:128]
    for j in range(5):
        stage1[j].wait_recv()
        p_snd2[j] = (p_keep1[j, 0:32] + p_rcv1[j, 0:32].astype(F32)).astype(BF)
        stage2.append(go(send(p_snd2.at[j], p_rcv2.at[j], ps_sem.at[1, j], pr_sem.at[1, j], pair_dev)))

    for cp in b_out:
        cp.wait_recv()
    for cp in loads[5:8]:
        cp.wait()
    for zz in range(8):
        cols = slice(zz * 640, (zz + 1) * 640)
        piece = jnp.concatenate([b_rcv3[qq, :, zz * 80:(zz + 1) * 80].astype(F32) for qq in range(8)], axis=1)
        base[:, cols] = res[:, cols].astype(F32) + gb[:, cols] * piece
    for j in range(5):
        cols = slice(j * 1024, (j + 1) * 1024)
        stage2[j].wait_recv()
        total = p_keep1[j, 32:64] + p_rcv1[j, 32:64].astype(F32) + p_rcv2[j].astype(F32)
        mixed_out[:, cols] = (base[:, cols] + ga[:, cols] * total).astype(BF)

    for cp in sent:
        cp.wait_send()
    for own, cp in back:
        @pl.when(jnp.logical_not(own))
        def _():
            cp.wait_send()


def window(q, k, v, res, ctx, wa, wb, ga, gb):
    any_space = pl.BlockSpec(memory_space=pl.ANY)
    vm = pl.BlockSpec(memory_space=pltpu.VMEM)
    D = pltpu.SemaphoreType.DMA
    V = pltpu.VMEM
    return pl.pallas_call(
        window_kernel,
        out_shape=(jax.ShapeDtypeStruct((32, 5120), BF), jax.ShapeDtypeStruct((128, 640), BF)),
        in_specs=[any_space] * 9,
        out_specs=(vm, vm),
        scratch_shapes=[
            V((32, 2560), BF), V((32, 2560), BF), V((32, 2560), BF), V((32, 5120), BF),
            V((640, 5120), BF), V((1, 5120), F32), V((1, 5120), F32),
            V((8, 3, 32, HD), BF), V((8, 2, 2, 32, HD), BF), V((4, 2, 32, HD), BF),
            V((4, 3, 8, 32, HD), BF),
            V((8, 2, 8, 2, 32, HD), BF), V((8, 4, 2, 32, HD), BF),
            V((3, 4, 1, 256), F32), V((3, 4, 1, 256), F32), V((3, 4, HD, 256), F32),
            V((4, 3, 2, HD, HD), BF), V((4, 3, 2, 8, HD), F32),
            V((4, 2, 2, HD, HD), BF), V((4, 2, HD, HD), BF), V((4, 2, 2, 8, HD), F32), V((4, 2, 8, HD), F32),
            V((2, 2, HD, HD), BF), V((HD, HD), BF), V((5, HD, HD), BF),
            V((8, 80, 640), BF), V((4, 2, HD, 640), BF), V((4, 2, 2, 2, 32, 640), BF), V((4, 2, 2, 32, 640), BF),
            V((2, 4, 32, 640), BF), V((2, 4, 32, 640), F32), V((2, 4, 32, 640), BF), V((2, 4, 32, 640), BF), V((4, 32, 640), BF),
            V((8, 32, 640), BF), V((32, 5120), F32),
            V((HD, 640), BF), V((HD, 5120), F32), V((5, 64, 1024), BF), V((5, 64, 1024), F32), V((5, 64, 1024), BF),
            V((5, 32, 1024), BF), V((5, 32, 1024), BF),
            D((9,)), D((4, 8)), D((4, 8)), D((4,)), D((4,)), D((3, 5, 2)), D((3, 5, 2)), D((4, 8)), D((4, 8)),
            D((5,)), D((5,)), D((5, 2)), D((5, 2)), D((8,)), D((8,)), D((9,)), D((9,)), D((2, 5)), D((2, 5)),
        ],
        compiler_params=pltpu.CompilerParams(collective_id=1, has_side_effects=True, vmem_limit_bytes=56 * 2**20),
        name="window",
    )(q, k, v, res, ctx, wa, wb.T, ga.reshape(1, 5120), gb.reshape(1, 5120))


def finish_kernel(mixed_in, cache_in, mixed_out, cache_out):
    mixed_out[...] = mixed_in[...]
    cache_out[...] = cache_in[...]


def finish(mixed, cache):
    vm = pl.BlockSpec(memory_space=pltpu.VMEM)
    return pl.pallas_call(
        finish_kernel,
        out_shape=(jax.ShapeDtypeStruct(mixed.shape, BF), jax.ShapeDtypeStruct(cache.shape, BF)),
        in_specs=[vm] * 2,
        out_specs=(vm, vm),
        name="finish",
    )(mixed, cache)


def on_device(*arrays):
    out = window(*arrays)
    return finish(*out)


def solution(mesh):
    tokens = P(("seq", "head"), None)
    return jax.shard_map(
        on_device,
        mesh=mesh,
        in_specs=(tokens, tokens, tokens, tokens, P("seq", "head"), P("head", None), P("head", "seq"), P(), P()),
        out_specs=(tokens, P("seq", "head")),
        check_vma=False,
    )
```

```python
import math

import jax
import jax.numpy as jnp
from jax import lax
from jax.experimental import pallas as pl
from jax.experimental.pallas import tpu as pltpu
from jax.sharding import PartitionSpec as P

MESH = pl.DeviceIdType.MESH
BF = jnp.bfloat16
F32 = jnp.float32
HD = 128
EXP2_SCALE = math.log2(math.e) / math.sqrt(HD)


def place():
    s, h = lax.axis_index("seq"), lax.axis_index("head")
    return (s // 4) % 2 * 2 + h // 2, s % 4, s // 8, h % 2


def device(x, y, z, c):
    return (z * 8 + x // 2 * 4 + y, x % 2 * 2 + c)


def send(src, dst, ssem, rsem, to):
    return pltpu.make_async_remote_copy(
        src_ref=src, dst_ref=dst, send_sem=ssem, recv_sem=rsem, device_id=to, device_id_type=MESH
    )


def window_kernel(
    q_hbm, k_hbm, v_hbm, res_hbm, ctx_hbm, wa_hbm, wb_hbm, ga_hbm, gb_hbm, mixed_out, cache_out,
    q_in, k_in, v_in, res, wa, ga, gb,
    q_pack, kv_pack, kvm_pack, q_buf, kv, kvm, m_ref, l_ref, ot, o_buf, st_buf, o_rcv, m_rcv, st_rcv, stm_rcv, c_res, m_res, attn, attn_far,
    w_all, ctx, b_part, b_rcv1, b_snd2, b_keep, b_rcv2, b_snd3, b_rcvx, b_rcv3, base,
    a_rows, p_pre, p_snd1, p_keep1, p_rcv1, p_snd2, p_rcv2,
    in_sem, xs_sem, xr_sem, ys_sem, yr_sem, zs_sem, zr_sem, os_sem, or_sem, bs_sem, br_sem,
    ws_sem, wr_sem, cs_sem, cr_sem, ds_sem, dr_sem, ps_sem, pr_sem,
):
    x, y, z, c = place()
    me = x * 2 + c
    xl, xh = x % 2, x // 2
    up, down = device(x, y, (z + 1) % 8, c), device(x, y, (z + 7) % 8, c)
    core_dev, pair_dev = device(x, y, z, 1 - c), device(xh * 2 + 1 - xl, y, z, c)
    far_x = (1 - xh) * 2 + xl
    x_peer = [None] + [(me + d) % 8 for d in range(1, 8)]
    x_dev = [None] + [device(p // 2, y, z, p % 2) for p in x_peer[1:]]
    sent = []

    def go(cp):
        cp.start()
        sent.append(cp)
        return cp

    loads = []
    for i, (src, dst) in enumerate((
        (k_hbm, k_in), (v_hbm, v_in), (q_hbm, q_in), (wb_hbm, w_all.at[z]), (ctx_hbm, ctx.at[0, 0]),
        (gb_hbm, gb), (res_hbm, res), (ga_hbm, ga), (wa_hbm, wa),
    )):
        loads.append(pltpu.make_async_copy(src, dst, in_sem.at[i]))
        if i < 8:
            loads[-1].start()

    barrier = pltpu.get_barrier_semaphore()
    peers = x_dev[1:] + [up, down]
    for d in range(1, 4):
        for cc in range(2):
            peers.append(device(x, (y + d) % 4, z, cc))
    for p in peers:
        pl.semaphore_signal(barrier, inc=1, device_id=p, device_id_type=MESH)

    for cp in loads[0:3]:
        cp.wait()
    for p in range(8):
        xx, cc = p // 2, p % 2
        heads = (5 * xx + 3 * cc, 5 * xx + 3 * cc + 1, 5 * xx + 2)
        for i, hh in enumerate(heads):
            cols = slice(hh * HD, (hh + 1) * HD)
            q_pack[p, i] = q_in[:, cols]
            if i < 2:
                kv_pack[p, i, 0] = k_in[:, cols]
                kv_pack[p, i, 1] = v_in[:, cols]
            elif cc == 0:
                kvm_pack[xx, 0] = k_in[:, cols]
                kvm_pack[xx, 1] = v_in[:, cols]
    q_buf[0, :, me] = q_pack[me]
    kv[0, :, me] = kv_pack[me]
    kvm[0, x] = kvm_pack[x]
    pl.semaphore_wait(barrier, len(peers))

    def w_ring(step, way):
        at = (z + 9 - step) % 8 if way == 0 else (z + 7 + step) % 8
        ref = w_all.at[at]
        if step == 4:
            ref = ref.at[0:48] if way == 0 else ref.at[48:80]
        return send(ref, ref, ws_sem.at[step, way], wr_sem.at[step, way], (up, down)[way])

    rings = {}

    def w_start(step):
        for way in range(2):
            rings[step, way] = go(w_ring(step, way))

    def w_wait(step):
        for way in range(2):
            rings[step, way].wait_recv()

    loads[3].wait()
    w_start(1)

    x_q = []

    def send_q():
        for d in range(1, 8):
            x_q.append(go(send(q_pack.at[x_peer[d]], q_buf.at[0, :, me], xs_sem.at[0, d], xr_sem.at[0, d], x_dev[d])))

    x_kv = [[], [], []]
    for i in range(2):
        for d in range(1, 8):
            x_kv[i].append(go(send(
                kv_pack.at[x_peer[d], i], kv.at[0, i, me], xs_sem.at[1 + i, d], xr_sem.at[1 + i, d], x_dev[d])))
    for d in range(1, 4):
        xx = (x + d) % 4
        x_kv[2].append(go(send(
            kvm_pack.at[xx], kvm.at[0, x], xs_sem.at[3, d], xr_sem.at[3, d], device(xx, y, z, c))))
    loads[8].start()
    send_q()
    ctx_y = []
    loads[4].wait()
    for d in range(1, 4):
        ctx_y.append(go(send(ctx.at[0, 0], ctx.at[0, d], cs_sem.at[d], cr_sem.at[d], device(x, (y + d) % 4, z, c))))
    w_wait(1)
    w_start(2)

    def part_ref(part, slot):
        return kvm.at[slot] if part == 2 else kv.at[slot, part]

    def ring(part, step, way):
        src = 0 if step == 1 else 2 * (step - 1) - 1 + way
        dst = 7 if step == 4 else 2 * step - 1 + way
        return send(
            part_ref(part, src), part_ref(part, dst), zs_sem.at[part, step, way], zr_sem.at[part, step, way], (up, down)[way])

    def ways_of(part, step):
        return (0, 1) if step < 4 else ((0,) if part == 0 else (1,))

    def ring_start(part, step):
        for way in ways_of(part, step):
            rings[part, step, way] = go(ring(part, step, way))

    def ring_next(part, step):
        for way in ways_of(part, step):
            rings[part, step, way].wait_recv()
        if step < 4:
            ring_start(part, step + 1)

    for part in range(3):
        for cp in x_kv[part]:
            cp.wait_recv()
        ring_start(part, 1)

    for cp in x_q:
        cp.wait_recv()
    y_q = []
    for d in range(1, 4):
        y_q.append(go(send(q_buf.at[0], q_buf.at[d], ys_sem.at[d], yr_sem.at[d], device(x, (y + d) % 4, z, c))))
    ctx_x = []
    for d in range(4):
        if d > 0:
            ctx_y[d - 1].wait_recv()
        ctx_x.append(go(send(ctx.at[0, d], ctx.at[1, d], cs_sem.at[4 + d], cr_sem.at[4 + d], device(far_x, y, z, c))))
    w_wait(2)
    w_start(3)

    def attend(head, lo, n, first=False, last=False):
        if head < 2:
            kk = kv[lo:lo + n, head, :, 0].reshape(n * 256, HD)
            vv = kv[lo:lo + n, head, :, 1].reshape(n * 256, HD)
        else:
            kk = kvm[lo:lo + n, :, 0].reshape(n * 128, HD)
            vv = kvm[lo:lo + n, :, 1].reshape(n * 128, HD)

        def scores(t):
            return lax.dot_general(
                kk, q_buf[t, head].reshape(256, HD), (((1,), (1,)), ((), ())), preferred_element_type=F32)

        def rest(t, s):
            top = jnp.max(s, axis=0, keepdims=True)
            if not first:
                old = m_ref[head, t]
                top = jnp.maximum(top, old)
                fade = jnp.exp2((old - top) * EXP2_SCALE)
            p = jnp.exp2(s * EXP2_SCALE - top * EXP2_SCALE)
            tot = jnp.sum(p, axis=0, keepdims=True)
            o = lax.dot_general(vv, p.astype(BF), (((0,), (0,)), ((), ())), preferred_element_type=F32)
            if not first:
                tot = l_ref[head, t] * fade + tot
                o = ot[head, t] * fade + o
            if last:
                o = (o * (1.0 / tot)).astype(BF)
                lse = top * EXP2_SCALE + jnp.log2(tot)
                for half in range(2):
                    cols = slice(half * HD, (half + 1) * HD)
                    o_buf[t, head, half] = o[:, cols]
                    st_buf[t, head, half, 0:1] = lse[:, cols]
            else:
                l_ref[head, t] = tot
                ot[head, t] = o
                m_ref[head, t] = top

        order = (1, 2, 3, 0)
        following = scores(order[0])
        for i, t in enumerate(order):
            current = following
            if i < 3:
                following = scores(order[i + 1])
            rest(t, current)

    b_core, b_pair = [], []

    def b_dot(e):
        def tile(i, _):
            part = lax.dot_general(
                ctx[e, pl.ds(2 * i, 2)].reshape(256, 640), w_all[...].reshape(640, 640),
                (((1,), (1,)), ((), ())), preferred_element_type=F32,
            )
            b_part[e, pl.ds(2 * i, 2)] = part.astype(BF).reshape(2, 2, 2, 32, 640)
            return 0
        lax.fori_loop(0, 2, tile, 0)
        b_core.append(go(send(b_part.at[e, :, :, 1 - c], b_rcv1.at[e], ds_sem.at[e], dr_sem.at[e], core_dev)))

    def b_sum1(e):
        b_core[e].wait_recv()

        def tile(d, _):
            b_snd2[e, d] = (b_part[e, d, 1 - xl, c].astype(F32) + b_rcv1[e, d, 1 - xl].astype(F32)).astype(BF)
            b_keep[e, d] = b_part[e, d, xl, c].astype(F32) + b_rcv1[e, d, xl].astype(F32)
            return 0
        lax.fori_loop(0, 4, tile, 0)
        b_pair.append(go(send(b_snd2.at[e], b_rcv2.at[e], ds_sem.at[2 + e], dr_sem.at[2 + e], pair_dev)))

    ring_next(0, 1)
    w_wait(3)
    w_start(4)
    ring_next(1, 1)
    ring_next(2, 1)
    w_wait(4)
    b_dot(0)
    ring_next(0, 2)
    for cp in y_q:
        cp.wait_recv()
    attend(0, 0, 3, first=True)
    ring_next(1, 2)
    attend(1, 0, 3, first=True)
    ring_next(2, 2)
    attend(2, 0, 3, first=True)
    b_sum1(0)
    attend(0, 3, 2)
    for cp in ctx_x:
        cp.wait_recv()
    b_dot(1)
    ring_next(0, 3)
    attend(1, 3, 2)
    ring_next(1, 3)
    attend(2, 3, 2)
    ring_next(2, 3)
    attend(0, 5, 2)
    b_sum1(1)
    attend(1, 5, 2)
    attend(2, 5, 2)

    outs = [[], [], []]
    for head in range(3):
        ring_next(head, 4)
        attend(head, 7, 1, last=True)
        for t in (1, 2, 3, 0):
            yy = (y + 4 - t) % 4
            same, other = device(x, yy, z, c), device(x, yy, z, 1 - c)

            def out(src, dst, i, to):
                outs[head].append(go(send(src, dst, os_sem.at[t, i], or_sem.at[t, i], to)))

            if head < 2 and t > 0:
                out(o_buf.at[t, head], o_rcv.at[t, head], 2 * head, same)
                out(st_buf.at[t, head], st_rcv.at[t, head], 2 * head + 1, same)
            elif head == 2:
                if t > 0:
                    out(o_buf.at[t, 2, c], m_rcv.at[t, 0], 4, same)
                    out(st_buf.at[t, 2, c], stm_rcv.at[t, 0], 5, same)
                out(o_buf.at[t, 2, 1 - c], m_rcv.at[t, 1], 6, other)
                out(st_buf.at[t, 2, 1 - c], stm_rcv.at[t, 1], 7, other)

    for e in range(2):
        b_pair[e].wait_recv()

    def b_sum2(d, _):
        for e in range(2):
            b_snd3[e, d] = (b_keep[e, d] + b_rcv2[e, d].astype(F32)).astype(BF)
        return 0
    lax.fori_loop(0, 4, b_sum2, 0)
    b_x = go(send(b_snd3.at[1], b_rcvx, ds_sem.at[4], dr_sem.at[4], device(far_x, y, z, c)))

    def merge(parts):
        top = parts[0][1]
        for _, s in parts[1:]:
            top = jnp.maximum(top, s)
        acc, tot = 0.0, 0.0
        for o, s in parts:
            w = jnp.exp2(s - top)
            acc = acc + o.astype(F32) * w
            tot = tot + w
        return (acc * (1.0 / tot)).T.astype(BF)

    back = []

    def give(src, dst, sem, to_x, rsem):
        own = (to_x == x) & (x % 2 == c)
        cp = send(src, dst, bs_sem.at[sem], br_sem.at[rsem], device(to_x, y, z, x % 2))
        loc = pltpu.make_async_copy(src, dst, br_sem.at[rsem])

        @pl.when(own)
        def _():
            loc.start()

        @pl.when(jnp.logical_not(own))
        def _():
            cp.start()
        back.append((own, cp))

    def give_rows(src, head, sem, half):
        give(src, attn.at[head], sem, 2 * half + x // 2, head)
        give(src.at[1 - x // 2, :, 1], attn_far.at[head], 5 + sem, 2 * (1 - half) + x // 2, 5 + head)

    for head in range(2):
        for cp in outs[head]:
            cp.wait_recv()
        for half in range(2):
            parts = [(o_buf[0, head, half], st_buf[0, head, half, 0:1])]
            for d in range(1, 4):
                parts.append((o_rcv[d, head, half], st_rcv[d, head, half, 0:1]))
            c_res[head, half] = merge(parts).reshape(2, 2, 2, 16, HD)
            give_rows(c_res.at[head, half], 3 * c + head, 2 * head + half, half)
    for cp in outs[2]:
        cp.wait_recv()
    parts = [(o_buf[0, 2, c], st_buf[0, 2, c, 0:1])]
    for d in range(4):
        if d > 0:
            parts.append((m_rcv[d, 0], stm_rcv[d, 0, 0:1]))
        parts.append((m_rcv[d, 1], stm_rcv[d, 1, 0:1]))
    m_res[...] = merge(parts).reshape(2, 2, 2, 16, HD)
    give_rows(m_res, 2, 4, c)

    b_x.wait_recv()
    q_me, q_far = xh * 4 + y, (1 - xh) * 4 + y
    b_out = []
    for d in range(1, 4):
        to = device(x, (y + 4 - d) % 4, z, c)
        b_out.append(go(send(b_snd3.at[0, d], b_rcv3.at[q_me], ds_sem.at[4 + d], dr_sem.at[4 + d], to)))
        b_out.append(go(send(b_rcvx.at[d], b_rcv3.at[q_far], ds_sem.at[7 + d], dr_sem.at[7 + d], to)))
    b_rcv3[q_me] = b_snd3[0, 0]
    b_rcv3[q_far] = b_rcvx[0]

    def take(head):
        pltpu.make_async_copy(m_res, attn.at[head], br_sem.at[head]).wait()
        pltpu.make_async_copy(m_res.at[0, :, 1], attn_far.at[head], br_sem.at[5 + head]).wait()
        cols = slice(head * HD, (head + 1) * HD)
        cache_out[:, cols] = attn[head].reshape(HD, HD)
        for i, row_c in enumerate((1 - c, c)):
            a_rows[i * 64:i * 64 + 32, cols] = attn[head, xl, row_c].reshape(32, HD)
            a_rows[i * 64 + 32:i * 64 + 48, cols] = attn[head, 1 - xl, row_c, 0]
            a_rows[i * 64 + 48:i * 64 + 64, cols] = attn_far[head, row_c]

    for head in (0, 1, 3, 4):
        take(head)
    loads[8].wait()
    for j in range(5):
        cols = slice(j * 1024, (j + 1) * 1024)
        p_pre[:, cols] = (
            jnp.dot(a_rows[:, 0:256], wa[0:256, cols], preferred_element_type=F32)
            + jnp.dot(a_rows[:, 384:640], wa[384:640, cols], preferred_element_type=F32)
        )
    take(2)
    stage1, stage2 = [], []
    for j in range(5):
        cols = slice(j * 1024, (j + 1) * 1024)
        part = jnp.dot(a_rows[:, 256:384], wa[256:384, cols], preferred_element_type=F32) + p_pre[:, cols]
        p_snd1[j] = part[0:64].astype(BF)
        stage1.append(go(send(p_snd1.at[j], p_rcv1.at[j], ps_sem.at[0, j], pr_sem.at[0, j], core_dev)))
        p_keep1[j] = part[64:128]
    for j in range(5):
        stage1[j].wait_recv()
        p_snd2[j] = (p_keep1[j, 32:64] + p_rcv1[j, 32:64].astype(F32)).astype(BF).reshape(2, 16, 1024)
        for i, to in enumerate((pair_dev, device(2 * (1 - xh) + 1 - xl, y, z, c))):
            stage2.append(go(send(p_snd2.at[j, i], p_rcv2.at[j, i], ps_sem.at[1 + i, j], pr_sem.at[1 + i, j], to)))

    for cp in b_out:
        cp.wait_recv()
    for cp in loads[5:8]:
        cp.wait()
    for zz in range(8):
        cols = slice(zz * 640, (zz + 1) * 640)
        piece = jnp.concatenate([b_rcv3[qq, :, zz * 80:(zz + 1) * 80].astype(F32) for qq in range(8)], axis=1)
        base[:, cols] = res[:, cols].astype(F32) + gb[:, cols] * piece
    for j in range(5):
        cols = slice(j * 1024, (j + 1) * 1024)
        for i in range(2):
            stage2[2 * j + i].wait_recv()
        total = p_keep1[j, 0:32] + p_rcv1[j, 0:32].astype(F32) + p_rcv2[j].reshape(32, 1024).astype(F32)
        mixed_out[:, cols] = (base[:, cols] + ga[:, cols] * total).astype(BF)

    for cp in sent:
        cp.wait_send()
    for own, cp in back:
        @pl.when(jnp.logical_not(own))
        def _():
            cp.wait_send()


def window(q, k, v, res, ctx, wa, wb, ga, gb):
    any_space = pl.BlockSpec(memory_space=pl.ANY)
    vm = pl.BlockSpec(memory_space=pltpu.VMEM)
    D = pltpu.SemaphoreType.DMA
    V = pltpu.VMEM
    return pl.pallas_call(
        window_kernel,
        out_shape=(jax.ShapeDtypeStruct((32, 5120), BF), jax.ShapeDtypeStruct((128, 640), BF)),
        in_specs=[any_space] * 9,
        out_specs=(vm, vm),
        scratch_shapes=[
            V((32, 2560), BF), V((32, 2560), BF), V((32, 2560), BF), V((32, 5120), BF),
            V((640, 5120), BF), V((1, 5120), F32), V((1, 5120), F32),
            V((8, 3, 32, HD), BF), V((8, 2, 2, 32, HD), BF), V((4, 2, 32, HD), BF),
            V((4, 3, 8, 32, HD), BF),
            V((8, 2, 8, 2, 32, HD), BF), V((8, 4, 2, 32, HD), BF),
            V((3, 4, 1, 256), F32), V((3, 4, 1, 256), F32), V((3, 4, HD, 256), F32),
            V((4, 3, 2, HD, HD), BF), V((4, 3, 2, 8, HD), F32),
            V((4, 2, 2, HD, HD), BF), V((4, 2, HD, HD), BF), V((4, 2, 2, 8, HD), F32), V((4, 2, 8, HD), F32),
            V((2, 2, 2, 2, 2, 16, HD), BF), V((2, 2, 2, 16, HD), BF), V((5, 2, 2, 2, 16, HD), BF), V((5, 2, 16, HD), BF),
            V((8, 80, 640), BF), V((2, 4, HD, 640), BF), V((2, 4, 2, 2, 32, 640), BF), V((2, 4, 2, 32, 640), BF),
            V((2, 4, 32, 640), BF), V((2, 4, 32, 640), F32), V((2, 4, 32, 640), BF), V((2, 4, 32, 640), BF), V((4, 32, 640), BF),
            V((8, 32, 640), BF), V((32, 5120), F32),
            V((HD, 640), BF), V((HD, 5120), F32), V((5, 64, 1024), BF), V((5, 64, 1024), F32), V((5, 64, 1024), BF),
            V((5, 2, 16, 1024), BF), V((5, 2, 16, 1024), BF),
            D((9,)), D((4, 8)), D((4, 8)), D((4,)), D((4,)), D((3, 5, 2)), D((3, 5, 2)), D((4, 8)), D((4, 8)),
            D((10,)), D((10,)), D((5, 2)), D((5, 2)), D((8,)), D((8,)), D((11,)), D((11,)), D((3, 5)), D((3, 5)),
        ],
        compiler_params=pltpu.CompilerParams(collective_id=1, has_side_effects=True, vmem_limit_bytes=56 * 2**20),
        name="window",
    )(q, k, v, res, ctx, wa, wb.T, ga.reshape(1, 5120), gb.reshape(1, 5120))


def finish_kernel(mixed_in, cache_in, mixed_out, cache_out):
    mixed_out[...] = mixed_in[...]
    cache_out[...] = cache_in[...]


def finish(mixed, cache):
    vm = pl.BlockSpec(memory_space=pltpu.VMEM)
    return pl.pallas_call(
        finish_kernel,
        out_shape=(jax.ShapeDtypeStruct(mixed.shape, BF), jax.ShapeDtypeStruct(cache.shape, BF)),
        in_specs=[vm] * 2,
        out_specs=(vm, vm),
        name="finish",
    )(mixed, cache)


def on_device(*arrays):
    out = window(*arrays)
    return finish(*out)


def solution(mesh):
    tokens = P(("seq", "head"), None)
    return jax.shard_map(
        on_device,
        mesh=mesh,
        in_specs=(tokens, tokens, tokens, tokens, P("seq", "head"), P("head", None), P("head", "seq"), P(), P()),
        out_specs=(tokens, P("seq", "head")),
        check_vma=False,
    )
```

```python
import math

import jax
import jax.numpy as jnp
from jax import lax
from jax.experimental import pallas as pl
from jax.experimental.pallas import tpu as pltpu
from jax.sharding import PartitionSpec as P

MESH = pl.DeviceIdType.MESH
BF = jnp.bfloat16
F32 = jnp.float32
HD = 128
EXP2_SCALE = math.log2(math.e) / math.sqrt(HD)


def place():
    s, h = lax.axis_index("seq"), lax.axis_index("head")
    return (s // 4) % 2 * 2 + h // 2, s % 4, s // 8, h % 2


def device(x, y, z, c):
    return (z * 8 + x // 2 * 4 + y, x % 2 * 2 + c)


def send(src, dst, ssem, rsem, to):
    return pltpu.make_async_remote_copy(
        src_ref=src, dst_ref=dst, send_sem=ssem, recv_sem=rsem, device_id=to, device_id_type=MESH
    )


def window_kernel(
    q_hbm, k_hbm, v_hbm, res_hbm, ctx_hbm, wa_hbm, wb_hbm, ga_hbm, gb_hbm, mixed_out, cache_out,
    q_in, k_in, v_in, res, wa, ga, gb,
    q_pack, kv_pack, kvm_pack, q_buf, kv, kvm, m_ref, l_ref, ot, o_buf, st_buf, o_rcv, m_rcv, st_rcv, stm_rcv, c_res, m_res, attn, attn_far,
    w_all, ctx, b_part, b_rcv1, b_snd2, b_keep, b_rcv2, b_snd3, b_rcvx, b_rcv3, base,
    a_rows, p_pre, p_snd1, p_keep1, p_rcv1, p_snd2, p_rcv2,
    in_sem, xs_sem, xr_sem, ys_sem, yr_sem, zs_sem, zr_sem, os_sem, or_sem, bs_sem, br_sem,
    ws_sem, wr_sem, cs_sem, cr_sem, ds_sem, dr_sem, ps_sem, pr_sem,
):
    x, y, z, c = place()
    me = x * 2 + c
    xl, xh = x % 2, x // 2
    up, down = device(x, y, (z + 1) % 8, c), device(x, y, (z + 7) % 8, c)
    core_dev, pair_dev = device(x, y, z, 1 - c), device(xh * 2 + 1 - xl, y, z, c)
    far_x = (1 - xh) * 2 + xl
    x_peer = [None] + [(me + d) % 8 for d in range(1, 8)]
    x_dev = [None] + [device(p // 2, y, z, p % 2) for p in x_peer[1:]]
    sent = []

    def go(cp):
        cp.start()
        sent.append(cp)
        return cp

    loads = []
    for i, (src, dst) in enumerate((
        (k_hbm, k_in), (v_hbm, v_in), (q_hbm, q_in), (wb_hbm, w_all.at[z]), (ctx_hbm, ctx.at[0, 0]),
        (gb_hbm, gb), (res_hbm, res), (ga_hbm, ga), (wa_hbm, wa),
    )):
        loads.append(pltpu.make_async_copy(src, dst, in_sem.at[i]))
        if i < 8:
            loads[-1].start()

    barrier = pltpu.get_barrier_semaphore()
    peers = x_dev[1:] + [up, down]
    for d in range(1, 4):
        for cc in range(2):
            peers.append(device(x, (y + d) % 4, z, cc))
    for p in peers:
        pl.semaphore_signal(barrier, inc=1, device_id=p, device_id_type=MESH)

    for cp in loads[0:3]:
        cp.wait()
    for p in range(8):
        xx, cc = p // 2, p % 2
        heads = (5 * xx + 3 * cc, 5 * xx + 3 * cc + 1, 5 * xx + 2)
        for i, hh in enumerate(heads):
            cols = slice(hh * HD, (hh + 1) * HD)
            q_pack[p, i] = q_in[:, cols]
            if i < 2:
                kv_pack[p, i, 0] = k_in[:, cols]
                kv_pack[p, i, 1] = v_in[:, cols]
            elif cc == 0:
                kvm_pack[xx, 0] = k_in[:, cols]
                kvm_pack[xx, 1] = v_in[:, cols]
    q_buf[0, :, me] = q_pack[me]
    kv[0, :, me] = kv_pack[me]
    kvm[0, x] = kvm_pack[x]
    pl.semaphore_wait(barrier, len(peers))

    def w_ring(step, way):
        at = (z + 9 - step) % 8 if way == 0 else (z + 7 + step) % 8
        ref = w_all.at[at]
        if step == 4:
            ref = ref.at[0:48] if way == 0 else ref.at[48:80]
        return send(ref, ref, ws_sem.at[step, way], wr_sem.at[step, way], (up, down)[way])

    rings = {}

    def w_start(step):
        for way in range(2):
            rings[step, way] = go(w_ring(step, way))

    def w_wait(step):
        for way in range(2):
            rings[step, way].wait_recv()

    loads[3].wait()
    w_start(1)

    x_q = []

    def send_q():
        for d in range(1, 8):
            x_q.append(go(send(q_pack.at[x_peer[d]], q_buf.at[0, :, me], xs_sem.at[0, d], xr_sem.at[0, d], x_dev[d])))

    x_kv = [[], [], []]
    for i in range(2):
        for d in range(1, 8):
            x_kv[i].append(go(send(
                kv_pack.at[x_peer[d], i], kv.at[0, i, me], xs_sem.at[1 + i, d], xr_sem.at[1 + i, d], x_dev[d])))
    for d in range(1, 4):
        xx = (x + d) % 4
        x_kv[2].append(go(send(
            kvm_pack.at[xx], kvm.at[0, x], xs_sem.at[3, d], xr_sem.at[3, d], device(xx, y, z, c))))
    loads[8].start()
    send_q()
    ctx_y = []
    loads[4].wait()
    for d in range(1, 4):
        ctx_y.append(go(send(ctx.at[0, 0], ctx.at[0, d], cs_sem.at[d], cr_sem.at[d], device(x, (y + d) % 4, z, c))))
    w_wait(1)
    w_start(2)

    def part_ref(part, slot):
        return kvm.at[slot] if part == 2 else kv.at[slot, part]

    def ring(part, step, way):
        src = 0 if step == 1 else 2 * (step - 1) - 1 + way
        dst = 7 if step == 4 else 2 * step - 1 + way
        return send(
            part_ref(part, src), part_ref(part, dst), zs_sem.at[part, step, way], zr_sem.at[part, step, way], (up, down)[way])

    def ways_of(part, step):
        return (0, 1) if step < 4 else ((0,) if part == 0 else (1,))

    def ring_start(part, step):
        for way in ways_of(part, step):
            rings[part, step, way] = go(ring(part, step, way))

    def ring_next(part, step):
        for way in ways_of(part, step):
            rings[part, step, way].wait_recv()
        if step < 4:
            ring_start(part, step + 1)

    for part in range(3):
        for cp in x_kv[part]:
            cp.wait_recv()
        ring_start(part, 1)

    for cp in x_q:
        cp.wait_recv()
    y_q = []
    for d in range(1, 4):
        y_q.append(go(send(q_buf.at[0], q_buf.at[d], ys_sem.at[d], yr_sem.at[d], device(x, (y + d) % 4, z, c))))
    ctx_x = []
    for d in range(4):
        if d > 0:
            ctx_y[d - 1].wait_recv()
        ctx_x.append(go(send(ctx.at[0, d], ctx.at[1, d], cs_sem.at[4 + d], cr_sem.at[4 + d], device(far_x, y, z, c))))
    w_wait(2)
    w_start(3)

    def attend(head, lo, n, first=False, last=False):
        if head < 2:
            kk = kv[lo:lo + n, head, :, 0].reshape(n * 256, HD)
            vv = kv[lo:lo + n, head, :, 1].reshape(n * 256, HD)
        else:
            kk = kvm[lo:lo + n, :, 0].reshape(n * 128, HD)
            vv = kvm[lo:lo + n, :, 1].reshape(n * 128, HD)

        def scores(t):
            return lax.dot_general(
                kk, q_buf[t, head].reshape(256, HD), (((1,), (1,)), ((), ())), preferred_element_type=F32)

        def rest(t, s):
            top = jnp.max(s, axis=0, keepdims=True)
            if not first:
                old = m_ref[head, t]
                top = jnp.maximum(top, old)
                fade = jnp.exp2((old - top) * EXP2_SCALE)
            p = jnp.exp2(s * EXP2_SCALE - top * EXP2_SCALE)
            tot = jnp.sum(p, axis=0, keepdims=True)
            o = lax.dot_general(vv, p.astype(BF), (((0,), (0,)), ((), ())), preferred_element_type=F32)
            if not first:
                tot = l_ref[head, t] * fade + tot
                o = ot[head, t] * fade + o
            if last:
                o = (o * (1.0 / tot)).astype(BF)
                lse = top * EXP2_SCALE + jnp.log2(tot)
                for half in range(2):
                    cols = slice(half * HD, (half + 1) * HD)
                    o_buf[t, head, half] = o[:, cols]
                    st_buf[t, head, half, 0:1] = lse[:, cols]
            else:
                l_ref[head, t] = tot
                ot[head, t] = o
                m_ref[head, t] = top

        order = (1, 2, 3, 0)
        following = scores(order[0])
        for i, t in enumerate(order):
            current = following
            if i < 3:
                following = scores(order[i + 1])
            rest(t, current)

    b_core, b_pair = [], []

    def b_dot(e):
        def tile(i, _):
            part = lax.dot_general(
                ctx[e, pl.ds(2 * i, 2)].reshape(256, 640), w_all[...].reshape(640, 640),
                (((1,), (1,)), ((), ())), preferred_element_type=F32,
            )
            b_part[e, pl.ds(2 * i, 2)] = part.astype(BF).reshape(2, 2, 2, 32, 640)
            return 0
        lax.fori_loop(0, 2, tile, 0)
        b_core.append(go(send(b_part.at[e, :, :, 1 - c], b_rcv1.at[e], ds_sem.at[e], dr_sem.at[e], core_dev)))

    def b_sum1(e):
        b_core[e].wait_recv()

        def tile(d, _):
            b_snd2[e, d] = (b_part[e, d, 1 - xl, c].astype(F32) + b_rcv1[e, d, 1 - xl].astype(F32)).astype(BF)
            b_keep[e, d] = b_part[e, d, xl, c].astype(F32) + b_rcv1[e, d, xl].astype(F32)
            return 0
        lax.fori_loop(0, 4, tile, 0)
        b_pair.append(go(send(b_snd2.at[e], b_rcv2.at[e], ds_sem.at[2 + e], dr_sem.at[2 + e], pair_dev)))

    ring_next(0, 1)
    w_wait(3)
    w_start(4)
    ring_next(1, 1)
    ring_next(2, 1)
    w_wait(4)
    b_dot(0)
    ring_next(0, 2)
    for cp in y_q:
        cp.wait_recv()
    attend(0, 0, 3, first=True)
    ring_next(1, 2)
    attend(1, 0, 3, first=True)
    ring_next(2, 2)
    attend(2, 0, 3, first=True)
    b_sum1(0)
    attend(0, 3, 2)
    for cp in ctx_x:
        cp.wait_recv()
    b_dot(1)
    ring_next(0, 3)
    attend(1, 3, 2)
    ring_next(1, 3)
    attend(2, 3, 2)
    ring_next(2, 3)
    attend(0, 5, 2)
    b_sum1(1)
    attend(1, 5, 2)
    attend(2, 5, 2)

    outs = [[], [], []]
    for head in range(3):
        ring_next(head, 4)
        attend(head, 7, 1, last=True)
        for t in (1, 2, 3, 0):
            yy = (y + 4 - t) % 4
            same, other = device(x, yy, z, c), device(x, yy, z, 1 - c)

            def out(src, dst, i, to):
                outs[head].append(go(send(src, dst, os_sem.at[t, i], or_sem.at[t, i], to)))

            if head < 2 and t > 0:
                out(o_buf.at[t, head], o_rcv.at[t, head], 2 * head, same)
                out(st_buf.at[t, head], st_rcv.at[t, head], 2 * head + 1, same)
            elif head == 2:
                if t > 0:
                    out(o_buf.at[t, 2, c], m_rcv.at[t, 0], 4, same)
                    out(st_buf.at[t, 2, c], stm_rcv.at[t, 0], 5, same)
                out(o_buf.at[t, 2, 1 - c], m_rcv.at[t, 1], 6, other)
                out(st_buf.at[t, 2, 1 - c], stm_rcv.at[t, 1], 7, other)

    for e in range(2):
        b_pair[e].wait_recv()

    def b_sum2(d, _):
        for e in range(2):
            b_snd3[e, d] = (b_keep[e, d] + b_rcv2[e, d].astype(F32)).astype(BF)
        return 0
    lax.fori_loop(0, 4, b_sum2, 0)
    b_x = go(send(b_snd3.at[1], b_rcvx, ds_sem.at[4], dr_sem.at[4], device(far_x, y, z, c)))

    def merge(parts):
        top = parts[0][1]
        for _, s in parts[1:]:
            top = jnp.maximum(top, s)
        acc, tot = 0.0, 0.0
        for o, s in parts:
            w = jnp.exp2(s - top)
            acc = acc + o.astype(F32) * w
            tot = tot + w
        return (acc * (1.0 / tot)).T.astype(BF)

    back = []

    def give(src, dst, sem, to_x, rsem):
        own = (to_x == x) & (x % 2 == c)
        cp = send(src, dst, bs_sem.at[sem], br_sem.at[rsem], device(to_x, y, z, x % 2))
        loc = pltpu.make_async_copy(src, dst, br_sem.at[rsem])

        @pl.when(own)
        def _():
            loc.start()

        @pl.when(jnp.logical_not(own))
        def _():
            cp.start()
        back.append((own, cp))

    def give_rows(src, head, sem, half):
        give(src, attn.at[head], sem, 2 * half + x // 2, head)
        give(src.at[1 - x // 2, :, 1], attn_far.at[head], 5 + sem, 2 * (1 - half) + x // 2, 5 + head)

    for head in range(2):
        for cp in outs[head]:
            cp.wait_recv()
        for half in range(2):
            parts = [(o_buf[0, head, half], st_buf[0, head, half, 0:1])]
            for d in range(1, 4):
                parts.append((o_rcv[d, head, half], st_rcv[d, head, half, 0:1]))
            c_res[head, half] = merge(parts).reshape(2, 2, 2, 16, HD)
            give_rows(c_res.at[head, half], 3 * c + head, 2 * head + half, half)
    for cp in outs[2]:
        cp.wait_recv()
    parts = [(o_buf[0, 2, c], st_buf[0, 2, c, 0:1])]
    for d in range(4):
        if d > 0:
            parts.append((m_rcv[d, 0], stm_rcv[d, 0, 0:1]))
        parts.append((m_rcv[d, 1], stm_rcv[d, 1, 0:1]))
    m_res[...] = merge(parts).reshape(2, 2, 2, 16, HD)
    give_rows(m_res, 2, 4, c)

    b_x.wait_recv()
    q_me, q_far = xh * 4 + y, (1 - xh) * 4 + y
    b_out = []
    for d in range(1, 4):
        to = device(x, (y + 4 - d) % 4, z, c)
        b_out.append(go(send(b_snd3.at[0, d], b_rcv3.at[q_me], ds_sem.at[4 + d], dr_sem.at[4 + d], to)))
        b_out.append(go(send(b_rcvx.at[d], b_rcv3.at[q_far], ds_sem.at[7 + d], dr_sem.at[7 + d], to)))
    b_rcv3[q_me] = b_snd3[0, 0]
    b_rcv3[q_far] = b_rcvx[0]

    def take(head):
        pltpu.make_async_copy(m_res, attn.at[head], br_sem.at[head]).wait()
        pltpu.make_async_copy(m_res.at[0, :, 1], attn_far.at[head], br_sem.at[5 + head]).wait()
        cols = slice(head * HD, (head + 1) * HD)
        cache_out[:, cols] = attn[head].reshape(HD, HD)
        for i, row_c in enumerate((1 - c, c)):
            a_rows[i * 64:i * 64 + 32, cols] = attn[head, xl, row_c].reshape(32, HD)
            a_rows[i * 64 + 32:i * 64 + 48, cols] = attn[head, 1 - xl, row_c, 0]
            a_rows[i * 64 + 48:i * 64 + 64, cols] = attn_far[head, row_c]

    for head in (0, 1, 3, 4):
        take(head)
    loads[8].wait()
    for j in range(5):
        cols = slice(j * 1024, (j + 1) * 1024)
        p_pre[:, cols] = (
            jnp.dot(a_rows[:, 0:256], wa[0:256, cols], preferred_element_type=F32)
            + jnp.dot(a_rows[:, 384:640], wa[384:640, cols], preferred_element_type=F32)
        )
    take(2)
    stage1, stage2 = [], []
    for j in range(5):
        cols = slice(j * 1024, (j + 1) * 1024)
        part = jnp.dot(a_rows[:, 256:384], wa[256:384, cols], preferred_element_type=F32) + p_pre[:, cols]
        p_snd1[j] = part[0:64].astype(BF)
        stage1.append(go(send(p_snd1.at[j], p_rcv1.at[j], ps_sem.at[0, j], pr_sem.at[0, j], core_dev)))
        p_keep1[j] = part[64:128]
    for j in range(5):
        stage1[j].wait_recv()
        p_snd2[j] = (p_keep1[j, 32:64] + p_rcv1[j, 32:64].astype(F32)).astype(BF).reshape(2, 16, 1024)
        for i, to in enumerate((pair_dev, device(2 * (1 - xh) + 1 - xl, y, z, c))):
            stage2.append(go(send(p_snd2.at[j, i], p_rcv2.at[j, i], ps_sem.at[1 + i, j], pr_sem.at[1 + i, j], to)))

    for cp in b_out:
        cp.wait_recv()
    for cp in loads[5:8]:
        cp.wait()
    for zz in range(8):
        cols = slice(zz * 640, (zz + 1) * 640)
        piece = jnp.concatenate([b_rcv3[qq, :, zz * 80:(zz + 1) * 80].astype(F32) for qq in range(8)], axis=1)
        base[:, cols] = res[:, cols].astype(F32) + gb[:, cols] * piece
    for j in range(5):
        cols = slice(j * 1024, (j + 1) * 1024)
        for i in range(2):
            stage2[2 * j + i].wait_recv()
        total = p_keep1[j, 0:32] + p_rcv1[j, 0:32].astype(F32) + p_rcv2[j].reshape(32, 1024).astype(F32)
        mixed_out[:, cols] = (base[:, cols] + ga[:, cols] * total).astype(BF)

    for cp in sent:
        cp.wait_send()
    for own, cp in back:
        @pl.when(jnp.logical_not(own))
        def _():
            cp.wait_send()


def window(q, k, v, res, ctx, wa, wb, ga, gb):
    any_space = pl.BlockSpec(memory_space=pl.ANY)
    vm = pl.BlockSpec(memory_space=pltpu.VMEM)
    D = pltpu.SemaphoreType.DMA
    V = pltpu.VMEM
    return pl.pallas_call(
        window_kernel,
        out_shape=(jax.ShapeDtypeStruct((32, 5120), BF), jax.ShapeDtypeStruct((128, 640), BF)),
        in_specs=[any_space] * 9,
        out_specs=(vm, vm),
        scratch_shapes=[
            V((32, 2560), BF), V((32, 2560), BF), V((32, 2560), BF), V((32, 5120), BF),
            V((640, 5120), BF), V((1, 5120), F32), V((1, 5120), F32),
            V((8, 3, 32, HD), BF), V((8, 2, 2, 32, HD), BF), V((4, 2, 32, HD), BF),
            V((4, 3, 8, 32, HD), BF),
            V((8, 2, 8, 2, 32, HD), BF), V((8, 4, 2, 32, HD), BF),
            V((3, 4, 1, 256), F32), V((3, 4, 1, 256), F32), V((3, 4, HD, 256), F32),
            V((4, 3, 2, HD, HD), BF), V((4, 3, 2, 8, HD), F32),
            V((4, 2, 2, HD, HD), BF), V((4, 2, HD, HD), BF), V((4, 2, 2, 8, HD), F32), V((4, 2, 8, HD), F32),
            V((2, 2, 2, 2, 2, 16, HD), BF), V((2, 2, 2, 16, HD), BF), V((5, 2, 2, 2, 16, HD), BF), V((5, 2, 16, HD), BF),
            V((8, 80, 640), BF), V((2, 4, HD, 640), BF), V((2, 4, 2, 2, 32, 640), BF), V((2, 4, 2, 32, 640), BF),
            V((2, 4, 32, 640), BF), V((2, 4, 32, 640), F32), V((2, 4, 32, 640), BF), V((2, 4, 32, 640), BF), V((4, 32, 640), BF),
            V((8, 32, 640), BF), V((32, 5120), F32),
            V((HD, 640), BF), V((HD, 5120), F32), V((5, 64, 1024), BF), V((5, 64, 1024), F32), V((5, 64, 1024), BF),
            V((5, 2, 16, 1024), BF), V((5, 2, 16, 1024), BF),
            D((9,)), D((4, 8)), D((4, 8)), D((4,)), D((4,)), D((3, 5, 2)), D((3, 5, 2)), D((4, 8)), D((4, 8)),
            D((10,)), D((10,)), D((5, 2)), D((5, 2)), D((8,)), D((8,)), D((11,)), D((11,)), D((3, 5)), D((3, 5)),
        ],
        compiler_params=pltpu.CompilerParams(collective_id=1, has_side_effects=True, vmem_limit_bytes=56 * 2**20),
        name="window",
    )(q, k, v, res, ctx, wa, wb.T, ga.reshape(1, 5120), gb.reshape(1, 5120))


def finish_kernel(mixed_in, cache_in, mixed_out, cache_out, mixed, cache, in_sem, out_sem):
    pieces = [(mixed_in.at[:, cols], mixed.at[:, cols], mixed_out.at[:, cols])
              for cols in (slice(0, 2560), slice(2560, 5120))] + [(cache_in, cache, cache_out)]
    reads = [pltpu.make_async_copy(src, mid, in_sem.at[i]) for i, (src, mid, _) in enumerate(pieces)]
    writes = [pltpu.make_async_copy(mid, dst, out_sem.at[i]) for i, (_, mid, dst) in enumerate(pieces)]
    for cp in reads:
        cp.start()
    for read, write in zip(reads, writes):
        read.wait()
        write.start()
    for cp in writes:
        cp.wait()


def finish(mixed, cache):
    any_space = pl.BlockSpec(memory_space=pl.ANY)
    return pl.pallas_call(
        finish_kernel,
        out_shape=(jax.ShapeDtypeStruct(mixed.shape, BF), jax.ShapeDtypeStruct(cache.shape, BF)),
        in_specs=[any_space] * 2,
        out_specs=(any_space, any_space),
        scratch_shapes=[
            pltpu.VMEM(mixed.shape, BF), pltpu.VMEM(cache.shape, BF),
            pltpu.SemaphoreType.DMA((3,)), pltpu.SemaphoreType.DMA((3,)),
        ],
        name="finish",
    )(mixed, cache)


def on_device(*arrays):
    out = window(*arrays)
    return finish(*out)


def solution(mesh):
    tokens = P(("seq", "head"), None)
    return jax.shard_map(
        on_device,
        mesh=mesh,
        in_specs=(tokens, tokens, tokens, tokens, P("seq", "head"), P("head", None), P("head", "seq"), P(), P()),
        out_specs=(tokens, P("seq", "head")),
        check_vma=False,
    )
```

```python
import math

import jax
import jax.numpy as jnp
from jax import lax
from jax.experimental import pallas as pl
from jax.experimental.pallas import tpu as pltpu
from jax.sharding import PartitionSpec as P

MESH = pl.DeviceIdType.MESH
BF = jnp.bfloat16
F32 = jnp.float32
HD = 128
EXP2_SCALE = math.log2(math.e) / math.sqrt(HD)


def place():
    s, h = lax.axis_index("seq"), lax.axis_index("head")
    return (s // 4) % 2 * 2 + h // 2, s % 4, s // 8, h % 2


def device(x, y, z, c):
    return (z * 8 + x // 2 * 4 + y, x % 2 * 2 + c)


def send(src, dst, ssem, rsem, to):
    return pltpu.make_async_remote_copy(
        src_ref=src, dst_ref=dst, send_sem=ssem, recv_sem=rsem, device_id=to, device_id_type=MESH
    )


def window_kernel(
    q_hbm, k_hbm, v_hbm, res_hbm, ctx_hbm, wa_hbm, wb_hbm, ga_hbm, gb_hbm, mixed_out, cache_out,
    q_in, k_in, v_in, res, wa, ga, gb,
    q_pack, kv_pack, kvm_pack, q_buf, kv, kvm, m_ref, l_ref, ot, o_buf, st_buf, o_rcv, m_rcv, st_rcv, stm_rcv, c_res, m_res, attn, attn_far,
    w_all, ctx, b_part, b_rcv1, b_snd2, b_keep, b_rcv2, b_snd3, b_rcvx, b_rcv3, base,
    a_rows, p_pre, p_snd1, p_keep1, p_rcv1, p_snd2, p_rcv2,
    in_sem, xs_sem, xr_sem, ys_sem, yr_sem, zs_sem, zr_sem, os_sem, or_sem, bs_sem, br_sem,
    ws_sem, wr_sem, cs_sem, cr_sem, ds_sem, dr_sem, ps_sem, pr_sem,
):
    x, y, z, c = place()
    me = x * 2 + c
    xl, xh = x % 2, x // 2
    up, down = device(x, y, (z + 1) % 8, c), device(x, y, (z + 7) % 8, c)
    core_dev, pair_dev = device(x, y, z, 1 - c), device(xh * 2 + 1 - xl, y, z, c)
    far_x = (1 - xh) * 2 + xl
    x_peer = [None] + [(me + d) % 8 for d in range(1, 8)]
    x_dev = [None] + [device(p // 2, y, z, p % 2) for p in x_peer[1:]]
    sent = []

    def go(cp):
        cp.start()
        sent.append(cp)
        return cp

    barrier = pltpu.get_barrier_semaphore()
    peers = x_dev[1:] + [up, down]
    for d in range(1, 4):
        for cc in range(2):
            peers.append(device(x, (y + d) % 4, z, cc))
    for p in peers:
        pl.semaphore_signal(barrier, inc=1, device_id=p, device_id_type=MESH)

    loads = []
    for i, (src, dst) in enumerate((
        (k_hbm, k_in), (v_hbm, v_in), (q_hbm, q_in), (wb_hbm, w_all.at[z]), (ctx_hbm, ctx.at[0, 0]),
        (gb_hbm, gb), (res_hbm, res), (ga_hbm, ga), (wa_hbm, wa),
    )):
        loads.append(pltpu.make_async_copy(src, dst, in_sem.at[i]))
        if i < 8:
            loads[-1].start()

    for cp in loads[0:2]:
        cp.wait()
    for p in range(8):
        xx, cc = p // 2, p % 2
        heads = (5 * xx + 3 * cc, 5 * xx + 3 * cc + 1, 5 * xx + 2)
        for i, hh in enumerate(heads):
            cols = slice(hh * HD, (hh + 1) * HD)
            if i < 2:
                kv_pack[p, i, 0] = k_in[:, cols]
                kv_pack[p, i, 1] = v_in[:, cols]
            elif cc == 0:
                kvm_pack[xx, 0] = k_in[:, cols]
                kvm_pack[xx, 1] = v_in[:, cols]
    kv[0, :, me] = kv_pack[me]
    kvm[0, x] = kvm_pack[x]
    pl.semaphore_wait(barrier, len(peers))

    def w_ring(step, way):
        at = (z + 9 - step) % 8 if way == 0 else (z + 7 + step) % 8
        ref = w_all.at[at]
        if step == 4:
            ref = ref.at[0:48] if way == 0 else ref.at[48:80]
        return send(ref, ref, ws_sem.at[step, way], wr_sem.at[step, way], (up, down)[way])

    rings = {}

    def w_start(step):
        for way in range(2):
            rings[step, way] = go(w_ring(step, way))

    def w_wait(step):
        for way in range(2):
            rings[step, way].wait_recv()

    loads[3].wait()
    w_start(1)

    x_q = []

    def send_q():
        loads[2].wait()
        for p in range(8):
            xx, cc = p // 2, p % 2
            for i, hh in enumerate((5 * xx + 3 * cc, 5 * xx + 3 * cc + 1, 5 * xx + 2)):
                q_pack[p, i] = q_in[:, hh * HD:(hh + 1) * HD]
        q_buf[0, :, me] = q_pack[me]
        for d in range(1, 8):
            x_q.append(go(send(q_pack.at[x_peer[d]], q_buf.at[0, :, me], xs_sem.at[0, d], xr_sem.at[0, d], x_dev[d])))

    x_kv = [[], [], []]
    for i in range(2):
        for d in range(1, 8):
            x_kv[i].append(go(send(
                kv_pack.at[x_peer[d], i], kv.at[0, i, me], xs_sem.at[1 + i, d], xr_sem.at[1 + i, d], x_dev[d])))
    for d in range(1, 4):
        xx = (x + d) % 4
        x_kv[2].append(go(send(
            kvm_pack.at[xx], kvm.at[0, x], xs_sem.at[3, d], xr_sem.at[3, d], device(xx, y, z, c))))
    loads[8].start()
    send_q()
    ctx_y = []
    loads[4].wait()
    for d in range(1, 4):
        ctx_y.append(go(send(ctx.at[0, 0], ctx.at[0, d], cs_sem.at[d], cr_sem.at[d], device(x, (y + d) % 4, z, c))))
    w_wait(1)
    w_start(2)

    def part_ref(part, slot):
        return kvm.at[slot] if part == 2 else kv.at[slot, part]

    def ring(part, step, way):
        src = 0 if step == 1 else 2 * (step - 1) - 1 + way
        dst = 7 if step == 4 else 2 * step - 1 + way
        return send(
            part_ref(part, src), part_ref(part, dst), zs_sem.at[part, step, way], zr_sem.at[part, step, way], (up, down)[way])

    def ways_of(part, step):
        return (0, 1) if step < 4 else ((0,) if part == 0 else (1,))

    def ring_start(part, step):
        for way in ways_of(part, step):
            rings[part, step, way] = go(ring(part, step, way))

    def ring_next(part, step):
        for way in ways_of(part, step):
            rings[part, step, way].wait_recv()
        if step < 4:
            ring_start(part, step + 1)

    for part in range(3):
        for cp in x_kv[part]:
            cp.wait_recv()
        ring_start(part, 1)

    for cp in x_q:
        cp.wait_recv()
    y_q = []
    for d in range(1, 4):
        y_q.append(go(send(q_buf.at[0], q_buf.at[d], ys_sem.at[d], yr_sem.at[d], device(x, (y + d) % 4, z, c))))
    ctx_x = []
    for d in range(4):
        if d > 0:
            ctx_y[d - 1].wait_recv()
        ctx_x.append(go(send(ctx.at[0, d], ctx.at[1, d], cs_sem.at[4 + d], cr_sem.at[4 + d], device(far_x, y, z, c))))
    w_wait(2)
    w_start(3)

    def attend(head, lo, n, first=False, last=False):
        if head < 2:
            kk = kv[lo:lo + n, head, :, 0].reshape(n * 256, HD)
            vv = kv[lo:lo + n, head, :, 1].reshape(n * 256, HD)
        else:
            kk = kvm[lo:lo + n, :, 0].reshape(n * 128, HD)
            vv = kvm[lo:lo + n, :, 1].reshape(n * 128, HD)

        def scores(t):
            return lax.dot_general(
                kk, q_buf[t, head].reshape(256, HD), (((1,), (1,)), ((), ())), preferred_element_type=F32)

        def rest(t, s):
            top = jnp.max(s, axis=0, keepdims=True)
            if not first:
                old = m_ref[head, t]
                top = jnp.maximum(top, old)
                fade = jnp.exp2((old - top) * EXP2_SCALE)
            p = jnp.exp2(s * EXP2_SCALE - top * EXP2_SCALE)
            tot = jnp.sum(p, axis=0, keepdims=True)
            o = lax.dot_general(vv, p.astype(BF), (((0,), (0,)), ((), ())), preferred_element_type=F32)
            if not first:
                tot = l_ref[head, t] * fade + tot
                o = ot[head, t] * fade + o
            if last:
                o = (o * (1.0 / tot)).astype(BF)
                lse = top * EXP2_SCALE + jnp.log2(tot)
                for half in range(2):
                    cols = slice(half * HD, (half + 1) * HD)
                    o_buf[t, head, half] = o[:, cols]
                    st_buf[t, head, half, 0:1] = lse[:, cols]
            else:
                l_ref[head, t] = tot
                ot[head, t] = o
                m_ref[head, t] = top

        order = (1, 2, 3, 0)
        following = scores(order[0])
        for i, t in enumerate(order):
            current = following
            if i < 3:
                following = scores(order[i + 1])
            rest(t, current)

    b_core, b_pair = [], []

    def b_dot(e):
        def tile(i, _):
            part = lax.dot_general(
                ctx[e, pl.ds(2 * i, 2)].reshape(256, 640), w_all[...].reshape(640, 640),
                (((1,), (1,)), ((), ())), preferred_element_type=F32,
            )
            b_part[e, pl.ds(2 * i, 2)] = part.astype(BF).reshape(2, 2, 2, 32, 640)
            return 0
        lax.fori_loop(0, 2, tile, 0)
        b_core.append(go(send(b_part.at[e, :, :, 1 - c], b_rcv1.at[e], ds_sem.at[e], dr_sem.at[e], core_dev)))

    def b_sum1(e):
        b_core[e].wait_recv()

        def tile(d, _):
            b_snd2[e, d] = (b_part[e, d, 1 - xl, c].astype(F32) + b_rcv1[e, d, 1 - xl].astype(F32)).astype(BF)
            b_keep[e, d] = b_part[e, d, xl, c].astype(F32) + b_rcv1[e, d, xl].astype(F32)
            return 0
        lax.fori_loop(0, 4, tile, 0)
        b_pair.append(go(send(b_snd2.at[e], b_rcv2.at[e], ds_sem.at[2 + e], dr_sem.at[2 + e], pair_dev)))

    ring_next(0, 1)
    w_wait(3)
    w_start(4)
    ring_next(1, 1)
    ring_next(2, 1)
    w_wait(4)
    b_dot(0)
    ring_next(0, 2)
    for cp in y_q:
        cp.wait_recv()
    attend(0, 0, 3, first=True)
    ring_next(1, 2)
    attend(1, 0, 3, first=True)
    ring_next(2, 2)
    attend(2, 0, 3, first=True)
    b_sum1(0)
    attend(0, 3, 2)
    for cp in ctx_x:
        cp.wait_recv()
    b_dot(1)
    ring_next(0, 3)
    attend(1, 3, 2)
    ring_next(1, 3)
    attend(2, 3, 2)
    ring_next(2, 3)
    attend(0, 5, 2)
    b_sum1(1)
    attend(1, 5, 2)
    attend(2, 5, 2)

    outs = [[], [], []]
    for head in range(3):
        ring_next(head, 4)
        attend(head, 7, 1, last=True)
        for t in (1, 2, 3, 0):
            yy = (y + 4 - t) % 4
            same, other = device(x, yy, z, c), device(x, yy, z, 1 - c)

            def out(src, dst, i, to):
                outs[head].append(go(send(src, dst, os_sem.at[t, i], or_sem.at[t, i], to)))

            if head < 2 and t > 0:
                out(o_buf.at[t, head], o_rcv.at[t, head], 2 * head, same)
                out(st_buf.at[t, head], st_rcv.at[t, head], 2 * head + 1, same)
            elif head == 2:
                if t > 0:
                    out(o_buf.at[t, 2, c], m_rcv.at[t, 0], 4, same)
                    out(st_buf.at[t, 2, c], stm_rcv.at[t, 0], 5, same)
                out(o_buf.at[t, 2, 1 - c], m_rcv.at[t, 1], 6, other)
                out(st_buf.at[t, 2, 1 - c], stm_rcv.at[t, 1], 7, other)

    for e in range(2):
        b_pair[e].wait_recv()

    def b_sum2(d, _):
        for e in range(2):
            b_snd3[e, d] = (b_keep[e, d] + b_rcv2[e, d].astype(F32)).astype(BF)
        return 0
    lax.fori_loop(0, 4, b_sum2, 0)
    b_x = go(send(b_snd3.at[1], b_rcvx, ds_sem.at[4], dr_sem.at[4], device(far_x, y, z, c)))

    def merge(parts):
        top = parts[0][1]
        for _, s in parts[1:]:
            top = jnp.maximum(top, s)
        acc, tot = 0.0, 0.0
        for o, s in parts:
            w = jnp.exp2(s - top)
            acc = acc + o.astype(F32) * w
            tot = tot + w
        return (acc * (1.0 / tot)).T.astype(BF)

    back = []

    def give(src, dst, sem, to_x, rsem):
        own = (to_x == x) & (x % 2 == c)
        cp = send(src, dst, bs_sem.at[sem], br_sem.at[rsem], device(to_x, y, z, x % 2))
        loc = pltpu.make_async_copy(src, dst, br_sem.at[rsem])

        @pl.when(own)
        def _():
            loc.start()

        @pl.when(jnp.logical_not(own))
        def _():
            cp.start()
        back.append((own, cp))

    def give_rows(src, head, sem, half):
        give(src, attn.at[head], sem, 2 * half + x // 2, head)
        give(src.at[1 - x // 2, :, 1], attn_far.at[head], 5 + sem, 2 * (1 - half) + x // 2, 5 + head)

    for head in range(2):
        for cp in outs[head]:
            cp.wait_recv()
        for half in range(2):
            parts = [(o_buf[0, head, half], st_buf[0, head, half, 0:1])]
            for d in range(1, 4):
                parts.append((o_rcv[d, head, half], st_rcv[d, head, half, 0:1]))
            c_res[head, half] = merge(parts).reshape(2, 2, 2, 16, HD)
            give_rows(c_res.at[head, half], 3 * c + head, 2 * head + half, half)
    for cp in outs[2]:
        cp.wait_recv()
    parts = [(o_buf[0, 2, c], st_buf[0, 2, c, 0:1])]
    for d in range(4):
        if d > 0:
            parts.append((m_rcv[d, 0], stm_rcv[d, 0, 0:1]))
        parts.append((m_rcv[d, 1], stm_rcv[d, 1, 0:1]))
    m_res[...] = merge(parts).reshape(2, 2, 2, 16, HD)
    give_rows(m_res, 2, 4, c)

    b_x.wait_recv()
    q_me, q_far = xh * 4 + y, (1 - xh) * 4 + y
    b_out = []
    for d in range(1, 4):
        to = device(x, (y + 4 - d) % 4, z, c)
        b_out.append(go(send(b_snd3.at[0, d], b_rcv3.at[q_me], ds_sem.at[4 + d], dr_sem.at[4 + d], to)))
        b_out.append(go(send(b_rcvx.at[d], b_rcv3.at[q_far], ds_sem.at[7 + d], dr_sem.at[7 + d], to)))
    b_rcv3[q_me] = b_snd3[0, 0]
    b_rcv3[q_far] = b_rcvx[0]

    def take(head):
        pltpu.make_async_copy(m_res, attn.at[head], br_sem.at[head]).wait()
        pltpu.make_async_copy(m_res.at[0, :, 1], attn_far.at[head], br_sem.at[5 + head]).wait()
        cols = slice(head * HD, (head + 1) * HD)
        cache_out[:, cols] = attn[head].reshape(HD, HD)
        for i, row_c in enumerate((1 - c, c)):
            a_rows[i * 64:i * 64 + 32, cols] = attn[head, xl, row_c].reshape(32, HD)
            a_rows[i * 64 + 32:i * 64 + 48, cols] = attn[head, 1 - xl, row_c, 0]
            a_rows[i * 64 + 48:i * 64 + 64, cols] = attn_far[head, row_c]

    for head in (0, 1, 3, 4):
        take(head)
    loads[8].wait()
    for j in range(2):
        cols = slice(j * 2560, (j + 1) * 2560)
        p_pre[:, cols] = (
            jnp.dot(a_rows[:, 0:256], wa[0:256, cols], preferred_element_type=F32)
            + jnp.dot(a_rows[:, 384:640], wa[384:640, cols], preferred_element_type=F32)
        )
    take(2)
    stage1, stage2 = [], []
    for j in range(2):
        cols = slice(j * 2560, (j + 1) * 2560)
        part = jnp.dot(a_rows[:, 256:384], wa[256:384, cols], preferred_element_type=F32) + p_pre[:, cols]
        p_snd1[j] = part[0:64].astype(BF)
        stage1.append(go(send(p_snd1.at[j], p_rcv1.at[j], ps_sem.at[0, j], pr_sem.at[0, j], core_dev)))
        p_keep1[j] = part[64:128]
    for j in range(2):
        stage1[j].wait_recv()
        p_snd2[j] = (p_keep1[j, 32:64] + p_rcv1[j, 32:64].astype(F32)).astype(BF).reshape(2, 16, 2560)
        for i, to in enumerate((pair_dev, device(2 * (1 - xh) + 1 - xl, y, z, c))):
            stage2.append(go(send(p_snd2.at[j, i], p_rcv2.at[j, i], ps_sem.at[1 + i, j], pr_sem.at[1 + i, j], to)))

    for cp in b_out:
        cp.wait_recv()
    for cp in loads[5:8]:
        cp.wait()
    for zz in range(8):
        cols = slice(zz * 640, (zz + 1) * 640)
        piece = jnp.concatenate([b_rcv3[qq, :, zz * 80:(zz + 1) * 80].astype(F32) for qq in range(8)], axis=1)
        base[:, cols] = res[:, cols].astype(F32) + gb[:, cols] * piece
    for j in range(2):
        cols = slice(j * 2560, (j + 1) * 2560)
        for i in range(2):
            stage2[2 * j + i].wait_recv()
        total = p_keep1[j, 0:32] + p_rcv1[j, 0:32].astype(F32) + p_rcv2[j].reshape(32, 2560).astype(F32)
        mixed_out[:, cols] = (base[:, cols] + ga[:, cols] * total).astype(BF)

    for cp in sent:
        cp.wait_send()
    for own, cp in back:
        @pl.when(jnp.logical_not(own))
        def _():
            cp.wait_send()


def window(q, k, v, res, ctx, wa, wb, ga, gb):
    any_space = pl.BlockSpec(memory_space=pl.ANY)
    vm = pl.BlockSpec(memory_space=pltpu.VMEM)
    D = pltpu.SemaphoreType.DMA
    V = pltpu.VMEM
    return pl.pallas_call(
        window_kernel,
        out_shape=(jax.ShapeDtypeStruct((32, 5120), BF), jax.ShapeDtypeStruct((128, 640), BF)),
        in_specs=[any_space] * 9,
        out_specs=(vm, vm),
        scratch_shapes=[
            V((32, 2560), BF), V((32, 2560), BF), V((32, 2560), BF), V((32, 5120), BF),
            V((640, 5120), BF), V((1, 5120), F32), V((1, 5120), F32),
            V((8, 3, 32, HD), BF), V((8, 2, 2, 32, HD), BF), V((4, 2, 32, HD), BF),
            V((4, 3, 8, 32, HD), BF),
            V((8, 2, 8, 2, 32, HD), BF), V((8, 4, 2, 32, HD), BF),
            V((3, 4, 1, 256), F32), V((3, 4, 1, 256), F32), V((3, 4, HD, 256), F32),
            V((4, 3, 2, HD, HD), BF), V((4, 3, 2, 8, HD), F32),
            V((4, 2, 2, HD, HD), BF), V((4, 2, HD, HD), BF), V((4, 2, 2, 8, HD), F32), V((4, 2, 8, HD), F32),
            V((2, 2, 2, 2, 2, 16, HD), BF), V((2, 2, 2, 16, HD), BF), V((5, 2, 2, 2, 16, HD), BF), V((5, 2, 16, HD), BF),
            V((8, 80, 640), BF), V((2, 4, HD, 640), BF), V((2, 4, 2, 2, 32, 640), BF), V((2, 4, 2, 32, 640), BF),
            V((2, 4, 32, 640), BF), V((2, 4, 32, 640), F32), V((2, 4, 32, 640), BF), V((2, 4, 32, 640), BF), V((4, 32, 640), BF),
            V((8, 32, 640), BF), V((32, 5120), F32),
            V((HD, 640), BF), V((HD, 5120), F32), V((2, 64, 2560), BF), V((2, 64, 2560), F32), V((2, 64, 2560), BF),
            V((2, 2, 16, 2560), BF), V((2, 2, 16, 2560), BF),
            D((9,)), D((4, 8)), D((4, 8)), D((4,)), D((4,)), D((3, 5, 2)), D((3, 5, 2)), D((4, 8)), D((4, 8)),
            D((10,)), D((10,)), D((5, 2)), D((5, 2)), D((8,)), D((8,)), D((11,)), D((11,)), D((3, 5)), D((3, 5)),
        ],
        compiler_params=pltpu.CompilerParams(collective_id=1, has_side_effects=True, vmem_limit_bytes=56 * 2**20),
        name="window",
    )(q, k, v, res, ctx, wa, wb.T, ga.reshape(1, 5120), gb.reshape(1, 5120))


def finish_kernel(mixed_in, cache_in, mixed_out, cache_out):
    mixed_out[...] = mixed_in[...]
    cache_out[...] = cache_in[...]


def finish(mixed, cache):
    vm = pl.BlockSpec(memory_space=pltpu.VMEM)
    return pl.pallas_call(
        finish_kernel,
        out_shape=(jax.ShapeDtypeStruct(mixed.shape, BF), jax.ShapeDtypeStruct(cache.shape, BF)),
        in_specs=[vm] * 2,
        out_specs=(vm, vm),
        name="finish",
    )(mixed, cache)


def on_device(*arrays):
    out = window(*arrays)
    return finish(*out)


def solution(mesh):
    tokens = P(("seq", "head"), None)
    return jax.shard_map(
        on_device,
        mesh=mesh,
        in_specs=(tokens, tokens, tokens, tokens, P("seq", "head"), P("head", None), P("head", "seq"), P(), P()),
        out_specs=(tokens, P("seq", "head")),
        check_vma=False,
    )
```
